256 devices in a mesh: dp: 16 (over z_lo, x), uly: 4 (over z_hi, core), blk: 4 (over y).
Axes of the slice: x: 4, y: 4, z: 8 (z_hi: 2, z_lo: 4; z = z_hi * 4 + z_lo), core: 2. Of those that a mesh axis runs over, the one named last changes fastest.
Arguments:
- query_rows: bfloat16 [16, 2048, 2560], P('dp', ('uly', 'blk')), may hold values from -6.5 to 6.5, as said below
- key_rows: bfloat16 [16, 2048, 2560], P('dp', ('uly', 'blk')), may hold values from -4 to 4, as said below
- value_rows: bfloat16 [16, 2048, 2560], P('dp', ('uly', 'blk')), may hold values from -6 to 6
- query_tangent: bfloat16 [16, 2048, 2560], P('dp', ('uly', 'blk')), may hold values from -6 to 6
- key_tangent: bfloat16 [16, 2048, 2560], P('dp', ('uly', 'blk')), may hold values from -6 to 6
- value_tangent: bfloat16 [16, 2048, 2560], P('dp', ('uly', 'blk')), may hold values from -6 to 6
- out_weight: bfloat16 [2560, 5120], P('uly', ('blk', 'dp')), may hold values from -0.125 to 0.125
Outputs:
- mixed: bfloat16 [16, 2048, 5120], P('dp', ('uly', 'blk'))
- mixed_tangent: bfloat16 [16, 2048, 5120], P('dp', ('uly', 'blk'))
The draws below stay inside these ranges and needn't reach their ends.
Inputs may be any that keep to these rules, and one draw needn't show every extreme that they name: `query_rows`: queries of unit-scale entries. `key_rows`: keys of unit-scale entries.
All inputs are finite; a program needn't handle non-finite values.
Results may differ from the reference program's by a relative error of at most 0.019.
Values may be sent and summed in bfloat16 or wider, within the bound.
A program may use at most 128 MiB of HBM per device.

```python
import jax
import jax.numpy as jnp
from jax import lax

D = 5120
HEAD_DIM = 128
HEADS = 20
HD = 2560
SEQ = 2048
CLIPS = 16
N_ULY = 4


def draw_query_rows(key, part):
    key = jax.random.fold_in(key, 11)
    base = jax.random.truncated_normal(key, -4.0, 4.0, (CLIPS, SEQ, HD), jnp.float32)
    return base.astype(jnp.bfloat16)


def draw_key_rows(key, part):
    key = jax.random.fold_in(key, 23)
    base = jax.random.truncated_normal(key, -4.0, 4.0, (CLIPS, SEQ, HD), jnp.float32)
    return base.astype(jnp.bfloat16)


def block_levels(key, shape, split, least, high):
    def one(axis_at, shards_of):
        steps = jax.random.uniform(jax.random.fold_in(jax.random.fold_in(key, 6), axis_at), (shards_of,), jnp.float32, least / len(split), high / len(split))
        return jnp.repeat(jnp.exp(steps), shape[axis_at] // shards_of).reshape((-1,) + (1,) * (len(shape) - axis_at - 1))

    level = one(*split[0])
    for cut in split[1:]:
        level = level * one(*cut)
    return level


def noise(stream_key, dims, scale, most, pieces=(), held_as=jnp.bfloat16):
    result = scale * jax.random.normal(stream_key, dims, jnp.float32)
    if pieces:
        result = result * block_levels(stream_key, dims, pieces, -0.22, 0.18)
    return jnp.clip(result, -most, most).astype(held_as)


def setup_inputs(seed: int = 0) -> dict:
    key_list = jax.random.split(jax.random.key(seed), 8)
    query_rows = draw_query_rows(jax.random.fold_in(key_list[7], 71), 0)
    key_rows = draw_key_rows(jax.random.fold_in(key_list[7], 71), 0)
    value_rows = noise(key_list[2], (CLIPS, SEQ, HD), 1.0, 6.0, ((0, 16), (1, 16)))
    query_tangent = noise(key_list[3], (CLIPS, SEQ, HD), 1.0, 6.0, ((0, 16), (1, 16)))
    key_tangent = noise(key_list[4], (CLIPS, SEQ, HD), 1.0, 6.0, ((0, 16), (1, 16)))
    value_tangent = noise(key_list[5], (CLIPS, SEQ, HD), 1.0, 6.0, ((0, 16), (1, 16)))
    out_weight = noise(key_list[6], (HD, D), HD ** -0.5, 0.125, ((0, 4), (1, 64)))
    return {"query_rows": query_rows, "key_rows": key_rows, "value_rows": value_rows, "query_tangent": query_tangent, "key_tangent": key_tangent, "value_tangent": value_tangent, "out_weight": out_weight}


def head_attention(items):
    query, key, value, query_tan, key_tan, value_tan = items
    factor = HEAD_DIM ** -0.5
    scores = jnp.dot(query, key.T, preferred_element_type=jnp.float32) * factor
    score_tan = (jnp.dot(query_tan, key.T, preferred_element_type=jnp.float32)
                 + jnp.dot(query, key_tan.T, preferred_element_type=jnp.float32)) * factor
    weights = jnp.exp(scores - jnp.max(scores, axis=1, keepdims=True))
    total = jnp.sum(weights, axis=1)
    spread = jnp.sum(weights * score_tan, axis=1)
    weights_low = weights.astype(jnp.bfloat16)
    moved_low = (weights * score_tan).astype(jnp.bfloat16)
    plain = jnp.dot(weights_low, value, preferred_element_type=jnp.float32)
    carried = (jnp.dot(moved_low, value, preferred_element_type=jnp.float32)
               + jnp.dot(weights_low, value_tan, preferred_element_type=jnp.float32))
    attended = plain / total[:, None]
    attended_tan = (carried - (spread / total)[:, None] * plain) / total[:, None]
    return attended.astype(jnp.bfloat16), attended_tan.astype(jnp.bfloat16)


def split_heads(array):
    return array.reshape(SEQ, HEADS, HEAD_DIM).transpose(1, 0, 2)


def one_clip(items, out_weight):
    heads = tuple(split_heads(item) for item in items)
    attended, attended_tan = lax.map(head_attention, heads)
    attended = attended.transpose(1, 0, 2).reshape(SEQ, HD)
    attended_tan = attended_tan.transpose(1, 0, 2).reshape(SEQ, HD)
    stacked = jnp.concatenate([attended, attended_tan], axis=0)
    group_width = HD // N_ULY
    summed = jnp.zeros((2 * SEQ, D), jnp.float32)
    for group in range(N_ULY):
        term = jnp.dot(stacked[:, group * group_width:(group + 1) * group_width],
                       out_weight[group * group_width:(group + 1) * group_width],
                       preferred_element_type=jnp.float32)
        term = lax.optimization_barrier(term.astype(jnp.bfloat16))
        summed = summed + term.astype(jnp.float32)
    summed = summed.astype(jnp.bfloat16)
    return summed[:SEQ], summed[SEQ:]


def reference(query_rows, key_rows, value_rows, query_tangent, key_tangent, value_tangent, out_weight):
    def clip_step(items):
        return one_clip(items, out_weight)

    mixed, mixed_tangent = lax.map(clip_step, (query_rows, key_rows, value_rows,
                                               query_tangent, key_tangent, value_tangent))
    return mixed, mixed_tangent
```

```python
import jax
import jax.numpy as jnp
from jax import lax
from jax.experimental import pallas as pl
from jax.experimental.pallas import tpu as pltpu
from jax.sharding import PartitionSpec as P

HEAD = 128
STEPS = 5
TOK = 128
SCALE = HEAD ** -0.5
LOG2E = 1.4426950408889634
MESH_IDS = pl.DeviceIdType.MESH
NT = (((1,), (1,)), ((), ()))
KEYS, VALUES, QUERIES = 0, 1, 2
COLUMN_ORDER = (0, 1, 3, 2)


def kernel(
    q_in, k_in, v_in, qt_in, kt_in, vt_in, w_in, out, out_t,
    kvb, qb, ob, ab, wt, acc, stage, wloc,
    a_send, a_recv, z_send, z_recv, c_send, c_recv, r_send, r_recv,
    wz_send, wz_recv, wy_send, wy_recv, wx_send, wx_recv, wd_send, wd_recv,
    l_sem, o_sem,
):
    dp = lax.axis_index("dp")
    uly = lax.axis_index("uly")
    y = lax.axis_index("blk")
    x = lax.rem(dp, 4)
    zl = lax.div(dp, 4)
    zh = lax.div(uly, 2)
    core = lax.rem(uly, 2)
    z = zh * 4 + zl

    def at_z(shift):
        there = lax.rem(z + shift + 8, 8)
        return {
            "dp": lax.rem(there, 4) * 4 + x,
            "uly": lax.div(there, 4) * 2 + core,
            "blk": y,
        }

    def at_y(shift):
        return {"dp": dp, "uly": uly, "blk": lax.rem(y + shift + 4, 4)}

    def at_x(shift):
        return {"dp": zl * 4 + lax.rem(x + shift + 4, 4), "uly": uly, "blk": y}

    other_core = {"dp": dp, "uly": zh * 2 + 1 - core, "blk": y}

    def remote(src, dst, send, recv, where):
        return pltpu.make_async_remote_copy(
            src_ref=src, dst_ref=dst, send_sem=send, recv_sem=recv,
            device_id=where, device_id_type=MESH_IDS,
        )

    def await_bytes(ref, sem):
        pltpu.make_async_copy(ref, ref, sem).wait()

    load_w = pltpu.make_async_copy(w_in, wloc, l_sem)
    load_w.start()

    partners = [at_y(1), at_y(2), at_y(3), at_x(1), at_x(-1), at_z(1), at_z(-1), at_z(4), other_core]
    barrier = pltpu.get_barrier_semaphore()
    for where in partners:
        pl.semaphore_signal(barrier, inc=1, device_id=where, device_id_type=MESH_IDS)
    pl.semaphore_wait(barrier, len(partners))

    pairs = ((k_in, kt_in), (v_in, vt_in), (q_in, qt_in))

    def landing(step, pair):
        if pair == QUERIES:
            return qb.at[step]
        return kvb.at[step, 0, 0, pl.ds(2 * pair, 2)]

    def heads_start(step, pair):
        land = landing(step, pair)
        for item in range(2):
            source = pairs[pair][item]
            for shift in (2, 1, 3, 0):
                owner = lax.rem(y + shift, 4)
                columns = pl.ds(pl.multiple_of(owner * (STEPS * HEAD) + step * HEAD, HEAD), HEAD)
                src = source.at[0, :, columns]
                if shift == 0:
                    pltpu.make_async_copy(src, land.at[item, 0], a_recv.at[step, pair]).start()
                else:
                    remote(src, land.at[item, shift], a_send.at[step, pair], a_recv.at[step, pair], at_y(shift)).start()

    def heads_wait(step, pair):
        await_bytes(landing(step, pair), a_recv.at[step, pair])

    def heads_sent(step, pair):
        if pair == QUERIES:
            await_bytes(qb.at[step, :, pl.ds(1, 3)], a_send.at[step, pair])
        else:
            await_bytes(kvb.at[step, 0, 0, pl.ds(2 * pair, 2), pl.ds(1, 3)], a_send.at[step, pair])

    def quarter(step, pair, rz, rc):
        return kvb.at[step, rz, rc, pl.ds(2 * pair, 2)]

    def z_copy(step, pair):
        half = 2 * step + pair
        return remote(quarter(step, pair, 0, 0), quarter(step, pair, 1, 0), z_send.at[half], z_recv.at[half], at_z(4))

    def core_copy(step, pair, rz):
        half = 2 * step + pair
        return remote(
            quarter(step, pair, rz, 0), quarter(step, pair, rz, 1),
            c_send.at[half, rz], c_recv.at[half, rz], other_core,
        )

    def spread_own(step):
        for pair in (KEYS, VALUES):
            heads_wait(step, pair)
            z_copy(step, pair).start()
            core_copy(step, pair, 0).start()

    def w_block(shift, rows):
        there = lax.rem(z + shift + 8, 8)
        return wt.at[lax.div(there, 4) * 2 + core, y, lax.rem(there, 4), x, rows]

    def wz_copy(ring, side):
        rows = pl.ds(0, 80)
        if ring == 3:
            rows = pl.ds(0, 48) if side == 1 else pl.ds(48, 32)
        src = w_block(-side * ring, rows)
        way = (side + 1) // 2
        return remote(src, src, wz_send.at[ring, way], wz_recv.at[ring, way], at_z(side))

    def group(rel_zh):
        return lax.rem(zh + rel_zh, 2) * 2 + core

    def wy_copy(rel_zh, ring, side):
        way = (side + 1) // 2
        if ring == 0:
            src = wt.at[group(rel_zh), y, :, x]
        else:
            there = lax.rem(y - side + 4, 4)
            src = wt.at[group(rel_zh), there, pl.ds(0, 2) if side == 1 else pl.ds(2, 2), x]
        return remote(src, src, wy_send.at[rel_zh, ring, way], wy_recv.at[rel_zh, ring, way], at_y(side))

    def unit_columns(unit):
        return lax.rem(y + COLUMN_ORDER[unit // 2], 4)

    def wx_copy(unit, ring, side):
        way = (side + 1) // 2
        if ring == 0:
            src = wt.at[group(unit % 2), unit_columns(unit), :, x]
        else:
            there = lax.rem(x - side + 4, 4)
            src = wt.at[group(unit % 2), unit_columns(unit), pl.ds(0, 2) if side == 1 else pl.ds(2, 2), there]
        return remote(src, src, wx_send.at[unit, ring, way], wx_recv.at[unit, ring, way], at_x(side))

    def wd_copy(unit):
        src = wt.at[group(unit % 2), unit_columns(unit)]
        return remote(src, src, wd_send.at[unit], wd_recv.at[unit], other_core)

    def both(make, *key):
        return [make(*key, side) for side in (1, -1)]

    def start(copies):
        for copy in copies:
            copy.start()

    def recv(copies):
        for copy in copies:
            copy.wait_recv()

    def recv_other_core(unit):
        src = wt.at[lax.rem(zh + unit % 2, 2) * 2 + 1 - core, unit_columns(unit)]
        await_bytes(src, wd_recv.at[unit])

    def attention(step):
        def block(index, carry):
            rows = pl.ds(index * 2, 2)
            query = qb[step, 0, rows].reshape(2 * TOK, HEAD)
            query_tan = qb[step, 1, rows].reshape(2 * TOK, HEAD)
            key, key_tan, value, value_tan = (
                kvb[step, :, :, item].reshape(16 * TOK, HEAD) for item in range(4)
            )
            scores = lax.dot_general(query, key, NT, preferred_element_type=jnp.float32)
            top = jnp.max(scores, axis=1, keepdims=True)
            weights = jnp.exp2((scores - top) * (SCALE * LOG2E))
            score_tan = lax.dot_general(
                jnp.concatenate([query_tan, query], axis=1),
                jnp.concatenate([key, key_tan], axis=1),
                NT, preferred_element_type=jnp.float32,
            )
            moved = weights * score_tan
            total = jnp.sum(weights, axis=1, keepdims=True)
            spread = jnp.sum(moved, axis=1, keepdims=True) * SCALE
            low = weights.astype(jnp.bfloat16)
            moved_low = moved.astype(jnp.bfloat16)
            sums = jnp.dot(low, jnp.concatenate([value, value_tan], axis=1), preferred_element_type=jnp.float32)
            plain = sums[:, :HEAD]
            carried = sums[:, HEAD:] + SCALE * jnp.dot(moved_low, value, preferred_element_type=jnp.float32)
            attended = plain / total
            attended_tan = (carried - (spread / total) * plain) / total
            ob[step, rows, 0] = attended.astype(jnp.bfloat16).reshape(2, TOK, HEAD)
            ob[step, rows, 1] = attended_tan.astype(jnp.bfloat16).reshape(2, TOK, HEAD)
            return carry

        lax.fori_loop(0, 2, block, 0)

    def home_copy(step, shift):
        return remote(ob.at[step, shift], ab.at[step, shift], r_send.at[step], r_recv.at[step], at_y(-shift))

    def home_start(step):
        start([home_copy(step, shift) for shift in (2, 1, 3)])

    def home_wait(step):
        await_bytes(ab.at[step, pl.ds(1, 3)], r_recv.at[step])

    def product(block, step):
        left = [ob[step, 0]] + [ab[step, shift] for shift in range(1, 4)]
        left = jnp.concatenate([item.reshape(2 * TOK, HEAD) for item in left], axis=1)
        lanes = pl.ds(pl.multiple_of(step * HEAD, HEAD), HEAD)
        right = jnp.concatenate(
            [wt[lax.rem(y + shift, 4), block, :, :, :, lanes].reshape(1280, HEAD) for shift in range(4)], axis=1
        )
        return lax.dot_general(left, right, NT, preferred_element_type=jnp.float32)

    def project(first, blocks, start_step, steps):
        def one(index, carry):
            rel = first + lax.div(index, steps)
            step = start_step + lax.rem(index, steps)
            shift = rel + lax.div(rel, 2) * (5 - 2 * rel)
            block = lax.rem(y + shift, 4)
            acc[block] += product(block, step)
            return carry

        lax.fori_loop(0, blocks * steps, one, 0)

    def out_copies(block):
        columns = pl.ds(pl.multiple_of(block * 1280, 1280), 1280)
        return [
            pltpu.make_async_copy(stage.at[block, pl.ds(item * TOK, TOK)], ref.at[0, :, columns], o_sem.at[block, item])
            for item, ref in enumerate((out, out_t))
        ]

    for pair in (KEYS, VALUES, QUERIES):
        heads_start(0, pair)
    load_w.wait()
    unit = (
        lax.broadcasted_iota(jnp.int32, (80, 80), 0) == lax.broadcasted_iota(jnp.int32, (80, 80), 1)
    ).astype(jnp.bfloat16)
    turned = lax.dot_general(unit, wloc[...], NT, preferred_element_type=jnp.float32)
    wt[uly, y, zl, x] = turned.astype(jnp.bfloat16)
    start(both(wz_copy, 0))
    spread_own(0)
    for pair in (KEYS, VALUES, QUERIES):
        heads_start(1, pair)
    acc[...] = jnp.zeros_like(acc)
    for ring in range(1, 4):
        recv(both(wz_copy, ring - 1))
        start(both(wz_copy, ring))
    recv(both(wz_copy, 3))
    for rel_zh in range(2):
        start(both(wx_copy, rel_zh, 0))
        start(both(wy_copy, rel_zh, 0))
    for step in range(1, STEPS):
        spread_own(step)
        if step + 1 < STEPS:
            for pair in (KEYS, VALUES, QUERIES):
                heads_start(step + 1, pair)

    for half in range(2 * STEPS):
        step, pair = half // 2, half % 2
        if half == 1:
            for rel_zh in range(2):
                recv(both(wy_copy, rel_zh, 0))
                start(both(wy_copy, rel_zh, 1))
            start(both(wx_copy, 2, 0))
            start(both(wx_copy, 3, 0))
        if 2 <= half <= 5:
            if half == 4:
                for rel_zh in range(2):
                    recv(both(wy_copy, rel_zh, 1))
            start(both(wx_copy, half + 2, 0))
        if half < 8:
            recv(both(wx_copy, half, 0))
            start(both(wx_copy, half, 1))
        if 1 <= half <= 8:
            recv(both(wx_copy, half - 1, 1))
            wd_copy(half - 1).start()
        if 2 <= half:
            recv_other_core(half - 2)
        if half == 8:
            home_wait(0)
            home_wait(1)
            home_wait(2)
            project(0, 3, 0, 3)
        if half == 9:
            home_wait(3)
            project(0, 3, 3, 1)
            project(3, 1, 0, 4)
            for other in range(STEPS):
                for kind in range(3):
                    heads_sent(other, kind)
                if other < 4:
                    await_bytes(ob.at[other, pl.ds(1, 3)], r_send.at[other])
            for other in range(8):
                for ring in range(2):
                    for copy in both(wx_copy, other, ring):
                        copy.wait_send()
                wd_copy(other).wait_send()
            for ring in range(4):
                for copy in both(wz_copy, ring):
                    copy.wait_send()
            for rel_zh in range(2):
                for ring in range(2):
                    for copy in both(wy_copy, rel_zh, ring):
                        copy.wait_send()
            for other in range(2 * STEPS):
                core_copy(other // 2, other % 2, 0).wait_send()
                if other < 9:
                    core_copy(other // 2, other % 2, 1).wait_send()
                    z_copy(other // 2, other % 2).wait_send()
        z_copy(step, pair).wait_recv()
        core_copy(step, pair, 1).start()
        if pair == VALUES:
            heads_wait(step, QUERIES)
            for kind in (KEYS, VALUES):
                for rz in range(2):
                    core_copy(step, kind, rz).wait_recv()
            attention(step)
            home_start(step)

    last = STEPS - 1
    home_wait(last)

    def finish(block, carry):
        stage[block] = (acc[block] + product(block, last)).astype(jnp.bfloat16)
        start(out_copies(block))
        return carry

    lax.fori_loop(0, 4, finish, 0)
    z_copy(last, VALUES).wait_send()
    core_copy(last, VALUES, 1).wait_send()
    await_bytes(ob.at[last, pl.ds(1, 3)], r_send.at[last])

    def drain(block, carry):
        for copy in out_copies(block):
            copy.wait()
        return carry

    lax.fori_loop(0, 4, drain, 0)


def per_device(*arrays):
    dma = pltpu.SemaphoreType.DMA
    low = jnp.bfloat16
    result = jax.ShapeDtypeStruct((1, TOK, 5120), low)
    anywhere = pl.BlockSpec(memory_space=pl.ANY)
    return pl.pallas_call(
        kernel,
        out_shape=(result, result),
        in_specs=[anywhere] * 7,
        out_specs=(anywhere, anywhere),
        scratch_shapes=[
            pltpu.VMEM((STEPS, 2, 2, 4, 4, TOK, HEAD), low),
            pltpu.VMEM((STEPS, 2, 4, TOK, HEAD), low),
            pltpu.VMEM((STEPS, 4, 2, TOK, HEAD), low),
            pltpu.VMEM((STEPS, 4, 2, TOK, HEAD), low),
            pltpu.VMEM((4, 4, 4, 4, 80, 640), low),
            pltpu.VMEM((4, 2 * TOK, 1280), jnp.float32),
            pltpu.VMEM((4, 2 * TOK, 1280), low),
            pltpu.VMEM((640, 80), low),
            dma((STEPS, 3)), dma((STEPS, 3)),
            dma((2 * STEPS,)), dma((2 * STEPS,)),
            dma((2 * STEPS, 2)), dma((2 * STEPS, 2)),
            dma((STEPS,)), dma((STEPS,)),
            dma((4, 2)), dma((4, 2)),
            dma((2, 2, 2)), dma((2, 2, 2)),
            dma((8, 2, 2)), dma((8, 2, 2)),
            dma((8,)), dma((8,)),
            dma, dma((4, 2)),
        ],
        compiler_params=pltpu.CompilerParams(
            collective_id=0, has_side_effects=True, vmem_limit_bytes=64 * 1024 * 1024
        ),
    )(*arrays)


def solution(mesh):
    rows = P("dp", ("uly", "blk"), None)
    return jax.shard_map(
        per_device,
        mesh=mesh,
        in_specs=(rows,) * 6 + (P("uly", ("blk", "dp")),),
        out_specs=(rows, rows),
        check_vma=False,
    )
```

```python
import jax
import jax.numpy as jnp
from jax import lax
from jax.experimental import pallas as pl
from jax.experimental.pallas import tpu as pltpu
from jax.sharding import PartitionSpec as P

HEAD = 128
STEPS = 5
TOK = 128
SCALE = HEAD ** -0.5
LOG2E = 1.4426950408889634
MESH_IDS = pl.DeviceIdType.MESH
NT = (((1,), (1,)), ((), ()))
KEYS, VALUES, QUERIES = 0, 1, 2
COLUMN_ORDER = (0, 1, 3, 2)


def kernel(
    q_in, k_in, v_in, qt_in, kt_in, vt_in, w_in, out, out_t, relay,
    kvb, qb, ob, ab, wt, acc, stage, low_ref, moved_ref, total_ref, spread_ref,
    a_send, a_recv, z_send, z_recv, c_send, c_recv, r_send, r_recv,
    wz_send, wz_recv, wy_send, wy_recv, wx_send, wx_recv, wd_send, wd_recv,
    xb_send, xb_recv, yb_send, yb_recv, db_send, db_recv,
    l_sem, o_sem,
):
    dp = lax.axis_index("dp")
    uly = lax.axis_index("uly")
    y = lax.axis_index("blk")
    x = lax.rem(dp, 4)
    zl = lax.div(dp, 4)
    zh = lax.div(uly, 2)
    core = lax.rem(uly, 2)
    z = zh * 4 + zl

    def at_z(shift):
        there = lax.rem(z + shift + 8, 8)
        return {
            "dp": lax.rem(there, 4) * 4 + x,
            "uly": lax.div(there, 4) * 2 + core,
            "blk": y,
        }

    def at_y(shift):
        return {"dp": dp, "uly": uly, "blk": lax.rem(y + shift + 4, 4)}

    def at_x(shift):
        return {"dp": zl * 4 + lax.rem(x + shift + 4, 4), "uly": uly, "blk": y}

    other_core = {"dp": dp, "uly": zh * 2 + 1 - core, "blk": y}

    def remote(src, dst, send, recv, where):
        return pltpu.make_async_remote_copy(
            src_ref=src, dst_ref=dst, send_sem=send, recv_sem=recv,
            device_id=where, device_id_type=MESH_IDS,
        )

    def await_bytes(ref, sem):
        pltpu.make_async_copy(ref, ref, sem).wait()

    load_w = pltpu.make_async_copy(w_in, wt.at[uly, y, zl, x], l_sem)
    load_w.start()

    partners = [at_y(1), at_y(2), at_y(3), at_x(1), at_x(-1), at_z(1), at_z(-1), other_core]
    barrier = pltpu.get_barrier_semaphore()
    for where in partners:
        pl.semaphore_signal(barrier, inc=1, device_id=where, device_id_type=MESH_IDS)
    pl.semaphore_wait(barrier, len(partners))

    pairs = ((k_in, kt_in), (v_in, vt_in), (q_in, qt_in))

    def landing(step, pair):
        if pair == QUERIES:
            return qb.at[step]
        return kvb.at[step, 0, 0, pl.ds(2 * pair, 2)]

    def heads_start(step, pair):
        land = landing(step, pair)
        for item in range(2):
            source = pairs[pair][item]
            for shift in (2, 1, 3, 0):
                owner = lax.rem(y + shift, 4)
                columns = pl.ds(pl.multiple_of(owner * (STEPS * HEAD) + step * HEAD, HEAD), HEAD)
                src = source.at[0, :, columns]
                if shift == 0:
                    pltpu.make_async_copy(src, land.at[item, 0], a_recv.at[step, pair]).start()
                else:
                    remote(src, land.at[item, shift], a_send.at[step, pair], a_recv.at[step, pair], at_y(shift)).start()

    def heads_wait(step, pair):
        await_bytes(landing(step, pair), a_recv.at[step, pair])

    def heads_sent(step, pair):
        if pair == QUERIES:
            await_bytes(qb.at[step, :, pl.ds(1, 3)], a_send.at[step, pair])
        else:
            await_bytes(kvb.at[step, 0, 0, pl.ds(2 * pair, 2), pl.ds(1, 3)], a_send.at[step, pair])

    def quarter(step, pair, rz, rc):
        return kvb.at[step, rz, rc, pl.ds(2 * pair, 2)]

    def z_copy(half, hop, way):
        step, pair = half // 2, half % 2
        src = kvb.at[step, 0, 0, 2 * pair + way] if hop == 1 else relay.at[half, hop - 2, way]
        dst = kvb.at[step, 1, 0, 2 * pair + way] if hop == 4 else relay.at[half, hop - 1, way]
        return remote(
            src, dst, z_send.at[half, hop - 1, way], z_recv.at[half, hop - 1, way], at_z(1 - 2 * way)
        )

    def z_copies(half, hop):
        return [z_copy(half, hop, way) for way in range(2)]

    def core_copy(step, pair, rz):
        half = 2 * step + pair
        return remote(
            quarter(step, pair, rz, 0), quarter(step, pair, rz, 1),
            c_send.at[half, rz], c_recv.at[half, rz], other_core,
        )

    def z_round(turn):
        for hop in (3, 2, 1):
            if 0 <= turn - hop < 2 * STEPS:
                recv(z_copies(turn - hop, hop))
                start(z_copies(turn - hop, hop + 1))
        if turn < 2 * STEPS:
            step, pair = turn // 2, turn % 2
            heads_wait(step, pair)
            start(z_copies(turn, 1))
            core_copy(step, pair, 0).start()

    def w_block(shift, rows):
        there = lax.rem(z + shift + 8, 8)
        return wt.at[lax.div(there, 4) * 2 + core, y, lax.rem(there, 4), x, rows]

    def wz_copy(ring, side):
        rows = pl.ds(0, 80)
        if ring == 3:
            rows = pl.ds(0, 48) if side == 1 else pl.ds(48, 32)
        dst = w_block(-side * ring, rows)
        way = (side + 1) // 2
        src = w_in if ring == 0 else dst
        return remote(src, dst, wz_send.at[ring, way], wz_recv.at[ring, way], at_z(side))

    def group(rel_zh):
        return lax.rem(zh + rel_zh, 2) * 2 + core

    first, rest = pl.ds(0, 3), 3

    def wy_copy(rel_zh, ring, side):
        way = (side + 1) // 2
        there = y if ring == 0 else lax.rem(y - side + 4, 4)
        src = wt.at[group(rel_zh), there, first, x]
        return remote(src, src, wy_send.at[rel_zh, ring, way], wy_recv.at[rel_zh, ring, way], at_y(side))

    def xb_copy(rel_zh, ring, side):
        way = (side + 1) // 2
        there = x if ring == 0 else lax.rem(x - side + 4, 4)
        src = wt.at[group(rel_zh), y, rest, there]
        return remote(src, src, xb_send.at[rel_zh, ring, way], xb_recv.at[rel_zh, ring, way], at_x(side))

    def yb_copy(rel_zh, ring, side):
        way = (side + 1) // 2
        there = y if ring == 0 else lax.rem(y - side + 4, 4)
        src = wt.at[group(rel_zh), there, rest]
        return remote(src, src, yb_send.at[rel_zh, ring, way], yb_recv.at[rel_zh, ring, way], at_y(side))

    def unit_columns(unit):
        return lax.rem(y + COLUMN_ORDER[unit // 2], 4)

    def wx_copy(unit, ring, side):
        way = (side + 1) // 2
        there = x if ring == 0 else lax.rem(x - side + 4, 4)
        src = wt.at[group(unit % 2), unit_columns(unit), first, there]
        return remote(src, src, wx_send.at[unit, ring, way], wx_recv.at[unit, ring, way], at_x(side))

    def wd_copy(unit):
        src = wt.at[group(unit % 2), unit_columns(unit), first]
        return remote(src, src, wd_send.at[unit], wd_recv.at[unit], other_core)

    def db_copy(unit):
        src = wt.at[group(unit % 2), unit_columns(unit), rest]
        return remote(src, src, db_send.at[unit], db_recv.at[unit], other_core)

    def both(make, *key):
        return [make(*key, side) for side in (1, -1)]

    def ring_of(make, index, ring):
        if ring == 0:
            return both(make, index, 0)
        return [make(index, 1, 1 if index % 2 == 0 else -1)]

    def start(copies):
        for copy in copies:
            copy.start()

    def recv(copies):
        for copy in copies:
            copy.wait_recv()

    def recv_other_core(unit):
        other_group = lax.rem(zh + unit % 2, 2) * 2 + 1 - core
        await_bytes(wt.at[other_group, unit_columns(unit), first], wd_recv.at[unit])

    def recv_other_rest(unit):
        other_group = lax.rem(zh + unit % 2, 2) * 2 + 1 - core
        await_bytes(wt.at[other_group, unit_columns(unit), rest], db_recv.at[unit])

    def weigh(step):
        def block(index, carry):
            rows = pl.ds(index * 2, 2)
            query = qb[step, 0, rows].reshape(2 * TOK, HEAD)
            query_tan = qb[step, 1, rows].reshape(2 * TOK, HEAD)
            key, key_tan = (kvb[step, :, :, item].reshape(16 * TOK, HEAD) for item in range(2))
            scores = lax.dot_general(query, key, NT, preferred_element_type=jnp.float32)
            top = jnp.max(scores, axis=1, keepdims=True)
            weights = jnp.exp2((scores - top) * (SCALE * LOG2E))
            score_tan = lax.dot_general(
                jnp.concatenate([query_tan, query], axis=1),
                jnp.concatenate([key, key_tan], axis=1),
                NT, preferred_element_type=jnp.float32,
            )
            moved = weights * score_tan
            total_ref[index] = jnp.sum(weights, axis=1, keepdims=True)
            spread_ref[index] = jnp.sum(moved, axis=1, keepdims=True) * SCALE
            low_ref[index] = weights.astype(jnp.bfloat16)
            moved_ref[index] = moved.astype(jnp.bfloat16)
            return carry

        lax.fori_loop(0, 2, block, 0)

    def attend(step):
        def block(index, carry):
            rows = pl.ds(index * 2, 2)
            value, value_tan = (kvb[step, :, :, item].reshape(16 * TOK, HEAD) for item in range(2, 4))
            total = total_ref[index]
            sums = jnp.dot(
                low_ref[index], jnp.concatenate([value, value_tan], axis=1), preferred_element_type=jnp.float32
            )
            plain = sums[:, :HEAD]
            carried = sums[:, HEAD:] + SCALE * jnp.dot(moved_ref[index], value, preferred_element_type=jnp.float32)
            attended = plain / total
            attended_tan = (carried - (spread_ref[index] / total) * plain) / total
            ob[step, rows, 0] = attended.astype(jnp.bfloat16).reshape(2, TOK, HEAD)
            ob[step, rows, 1] = attended_tan.astype(jnp.bfloat16).reshape(2, TOK, HEAD)
            return carry

        lax.fori_loop(0, 2, block, 0)

    def home_copy(step, shift):
        return remote(ob.at[step, shift], ab.at[step, shift], r_send.at[step], r_recv.at[step], at_y(-shift))

    def home_start(step):
        start([home_copy(step, shift) for shift in (2, 1, 3)])

    def home_wait(step):
        await_bytes(ab.at[step, pl.ds(1, 3)], r_recv.at[step])

    def product(block, step):
        left = [ob[step, 0]] + [ab[step, shift] for shift in range(1, 4)]
        left = jnp.concatenate([item.reshape(2 * TOK, HEAD) for item in left], axis=1)
        lanes = pl.ds(pl.multiple_of(step * HEAD, HEAD), HEAD)
        right = jnp.concatenate(
            [wt[lax.rem(y + shift, 4), block, :, :, :, lanes].reshape(1280, HEAD) for shift in range(4)], axis=1
        )
        return lax.dot_general(left, right, NT, preferred_element_type=jnp.float32)

    def project(first, blocks, start_step, steps):
        def one(index, carry):
            rel = first + lax.div(index, steps)
            step = start_step + lax.rem(index, steps)
            shift = rel + lax.div(rel, 2) * (5 - 2 * rel)
            block = lax.rem(y + shift, 4)
            acc[block] += product(block, step)
            return carry

        lax.fori_loop(0, blocks * steps, one, 0)

    def out_copies(block):
        columns = pl.ds(pl.multiple_of(block * 1280, 1280), 1280)
        return [
            pltpu.make_async_copy(stage.at[block, pl.ds(item * TOK, TOK)], ref.at[0, :, columns], o_sem.at[block, item])
            for item, ref in enumerate((out, out_t))
        ]

    def heads_of(step):
        for pair in (KEYS, VALUES, QUERIES):
            heads_start(step, pair)

    def sends_done():
        for step in range(STEPS):
            for kind in range(3):
                heads_sent(step, kind)
            if step < 4:
                await_bytes(ob.at[step, pl.ds(1, 3)], r_send.at[step])
        copies = []
        for unit in range(8):
            for ring in range(2):
                copies += ring_of(wx_copy, unit, ring)
            copies += [wd_copy(unit), db_copy(unit)]
        for ring in range(4):
            copies += both(wz_copy, ring)
        for rel_zh in range(2):
            for ring in range(2):
                for make in (wy_copy, xb_copy, yb_copy):
                    copies += ring_of(make, rel_zh, ring)
        for half in range(2 * STEPS):
            copies.append(core_copy(half // 2, half % 2, 0))
            for hop in range(1, 5):
                copies += z_copies(half, hop)
            if half < 9:
                copies.append(core_copy(half // 2, half % 2, 1))
        for copy in copies:
            copy.wait_send()

    def x_forward(unit):
        recv(ring_of(wx_copy, unit, 0))
        start(ring_of(wx_copy, unit, 1))
        if 2 <= unit + 2 <= 7:
            start(ring_of(wx_copy, unit + 2, 0))

    def x_done(unit):
        recv(ring_of(wx_copy, unit, 1))
        wd_copy(unit).start()

    def z_arrived(half):
        step, pair = half // 2, half % 2
        recv(z_copies(half, 4))
        core_copy(step, pair, 1).start()
        if pair == KEYS:
            heads_wait(step, QUERIES)
        core_copy(step, pair, 0).wait_recv()
        core_copy(step, pair, 1).wait_recv()
        if pair == KEYS:
            weigh(step)
        else:
            attend(step)
            home_start(step)

    def y_ring(make, ring):
        for rel_zh in range(2):
            start(ring_of(make, rel_zh, ring))

    def y_recv(make, ring):
        for rel_zh in range(2):
            recv(ring_of(make, rel_zh, ring))

    start(both(wz_copy, 0))
    heads_of(0)
    acc[...] = jnp.zeros_like(acc)
    heads_of(1)
    recv(both(wz_copy, 0))
    start(both(wz_copy, 1))
    z_round(0)
    recv(both(wz_copy, 1))
    start(both(wz_copy, 2))
    z_round(1)
    recv(both(wz_copy, 2))
    start(both(wz_copy, 3))
    z_round(2)
    recv(both(wz_copy, 3))
    load_w.wait()
    start(ring_of(wx_copy, 0, 0))
    y_ring(wy_copy, 0)
    y_ring(xb_copy, 0)
    start(ring_of(wx_copy, 1, 0))
    heads_of(2)
    z_round(3)
    y_recv(wy_copy, 0)
    x_forward(0)
    heads_of(3)
    y_ring(wy_copy, 1)
    z_round(4)
    y_recv(xb_copy, 0)
    y_ring(xb_copy, 1)
    x_forward(1)
    x_done(0)
    z_arrived(0)
    z_round(5)
    x_forward(2)
    x_done(1)
    heads_of(4)
    y_recv(xb_copy, 1)
    y_recv(wy_copy, 1)
    db_copy(0).start()
    db_copy(1).start()
    z_arrived(1)
    z_round(6)
    y_ring(yb_copy, 0)
    x_forward(3)
    x_done(2)
    z_arrived(2)
    z_round(7)
    x_forward(4)
    x_done(3)
    z_arrived(3)
    z_round(8)
    x_forward(5)
    x_done(4)
    y_recv(yb_copy, 0)
    y_ring(yb_copy, 1)
    for unit in range(2, 6):
        db_copy(unit).start()
    z_arrived(4)
    z_round(9)
    x_forward(6)
    x_done(5)
    z_arrived(5)
    z_round(10)
    x_forward(7)
    x_done(6)
    y_recv(yb_copy, 1)
    db_copy(6).start()
    db_copy(7).start()
    for unit in range(6):
        recv_other_core(unit)
        recv_other_rest(unit)
    for step in range(2):
        home_wait(step)
    project(0, 3, 0, 2)
    z_arrived(6)
    z_round(11)
    x_done(7)
    home_wait(2)
    project(0, 3, 2, 1)
    z_arrived(7)
    z_round(12)
    for unit in range(6, 8):
        recv_other_core(unit)
        recv_other_rest(unit)
    project(3, 1, 0, 3)
    z_arrived(8)
    home_wait(3)
    project(0, 4, 3, 1)
    sends_done()
    z_arrived(9)

    last = STEPS - 1
    home_wait(last)

    def finish(block, carry):
        stage[block] = (acc[block] + product(block, last)).astype(jnp.bfloat16)
        start(out_copies(block))
        return carry

    lax.fori_loop(0, 4, finish, 0)
    core_copy(last, VALUES, 1).wait_send()
    await_bytes(ob.at[last, pl.ds(1, 3)], r_send.at[last])

    def drain(block, carry):
        for copy in out_copies(block):
            copy.wait()
        return carry

    lax.fori_loop(0, 4, drain, 0)


def per_device(*arrays):
    dma = pltpu.SemaphoreType.DMA
    low = jnp.bfloat16
    result = jax.ShapeDtypeStruct((1, TOK, 5120), low)
    anywhere = pl.BlockSpec(memory_space=pl.ANY)
    return pl.pallas_call(
        kernel,
        out_shape=(result, result, jax.ShapeDtypeStruct((2 * STEPS, 3, 2, 4, TOK, HEAD), low)),
        in_specs=[anywhere] * 7,
        out_specs=(anywhere, anywhere, anywhere),
        scratch_shapes=[
            pltpu.VMEM((STEPS, 2, 2, 4, 4, TOK, HEAD), low),
            pltpu.VMEM((STEPS, 2, 4, TOK, HEAD), low),
            pltpu.VMEM((STEPS, 4, 2, TOK, HEAD), low),
            pltpu.VMEM((STEPS, 4, 2, TOK, HEAD), low),
            pltpu.VMEM((4, 4, 4, 4, 80, 640), low),
            pltpu.VMEM((4, 2 * TOK, 1280), jnp.float32),
            pltpu.VMEM((4, 2 * TOK, 1280), low),
            pltpu.VMEM((2, 2 * TOK, 16 * TOK), low),
            pltpu.VMEM((2, 2 * TOK, 16 * TOK), low),
            pltpu.VMEM((2, 2 * TOK, 1), jnp.float32),
            pltpu.VMEM((2, 2 * TOK, 1), jnp.float32),
            dma((STEPS, 3)), dma((STEPS, 3)),
            dma((2 * STEPS, 4, 2)), dma((2 * STEPS, 4, 2)),
            dma((2 * STEPS, 2)), dma((2 * STEPS, 2)),
            dma((STEPS,)), dma((STEPS,)),
            dma((4, 2)), dma((4, 2)),
            dma((2, 2, 2)), dma((2, 2, 2)),
            dma((8, 2, 2)), dma((8, 2, 2)),
            dma((8,)), dma((8,)),
            dma((2, 2, 2)), dma((2, 2, 2)),
            dma((2, 2, 2)), dma((2, 2, 2)),
            dma((8,)), dma((8,)),
            dma, dma((4, 2)),
        ],
        compiler_params=pltpu.CompilerParams(
            collective_id=0, has_side_effects=True, vmem_limit_bytes=64 * 1024 * 1024
        ),
    )(*arrays[:6], arrays[6].T)[:2]


def solution(mesh):
    rows = P("dp", ("uly", "blk"), None)
    return jax.shard_map(
        per_device,
        mesh=mesh,
        in_specs=(rows,) * 6 + (P("uly", ("blk", "dp")),),
        out_specs=(rows, rows),
        check_vma=False,
    )
```

```python
import jax
import jax.numpy as jnp
from jax import lax
from jax.experimental import pallas as pl
from jax.experimental.pallas import tpu as pltpu
from jax.sharding import PartitionSpec as P

HEAD = 128
STEPS = 5
TOK = 128
SCALE = HEAD ** -0.5
LOG2E = 1.4426950408889634
MESH_IDS = pl.DeviceIdType.MESH
NT = (((1,), (1,)), ((), ()))
KEYS, VALUES, QUERIES = 0, 1, 2
COLUMN_ORDER = (0, 1, 3, 2)


def kernel(
    q_in, k_in, v_in, qt_in, kt_in, vt_in, w_in, out, out_t,
    relay, kvb, qb, ob, ab, wt, acc, stage, low_ref, moved_ref, total_ref, spread_ref, sums_ref, carry_ref,
    a_send, a_recv, z_send, z_recv, c_send, c_recv, r_send, r_recv,
    wz_send, wz_recv, wy_send, wy_recv, wx_send, wx_recv, wd_send, wd_recv,
    xb_send, xb_recv, yb_send, yb_recv, db_send, db_recv,
    l_sem, o_sem,
):
    dp = lax.axis_index("dp")
    uly = lax.axis_index("uly")
    y = lax.axis_index("blk")
    x = lax.rem(dp, 4)
    zl = lax.div(dp, 4)
    zh = lax.div(uly, 2)
    core = lax.rem(uly, 2)
    z = zh * 4 + zl

    def at_z(shift):
        there = lax.rem(z + shift + 8, 8)
        return {
            "dp": lax.rem(there, 4) * 4 + x,
            "uly": lax.div(there, 4) * 2 + core,
            "blk": y,
        }

    def at_y(shift):
        return {"dp": dp, "uly": uly, "blk": lax.rem(y + shift + 4, 4)}

    def at_x(shift):
        return {"dp": zl * 4 + lax.rem(x + shift + 4, 4), "uly": uly, "blk": y}

    other_core = {"dp": dp, "uly": zh * 2 + 1 - core, "blk": y}

    def remote(src, dst, send, recv, where):
        return pltpu.make_async_remote_copy(
            src_ref=src, dst_ref=dst, send_sem=send, recv_sem=recv,
            device_id=where, device_id_type=MESH_IDS,
        )

    def await_bytes(ref, sem):
        pltpu.make_async_copy(ref, ref, sem).wait()

    load_w = pltpu.make_async_copy(w_in, wt.at[uly, y, zl, x], l_sem)
    load_w.start()

    partners = [at_y(1), at_y(2), at_y(3), at_x(1), at_x(-1), at_z(1), at_z(-1), other_core]
    barrier = pltpu.get_barrier_semaphore()
    for where in partners:
        pl.semaphore_signal(barrier, inc=1, device_id=where, device_id_type=MESH_IDS)
    pl.semaphore_wait(barrier, len(partners))

    pairs = ((k_in, kt_in), (v_in, vt_in), (q_in, qt_in))

    def landing(step, pair):
        if pair == QUERIES:
            return qb.at[step]
        return kvb.at[step, 0, 0, pl.ds(2 * pair, 2)]

    def heads_start(step, pair):
        land = landing(step, pair)
        for item in range(2):
            source = pairs[pair][item]
            for shift in (2, 1, 3, 0):
                owner = lax.rem(y + shift, 4)
                columns = pl.ds(pl.multiple_of(owner * (STEPS * HEAD) + step * HEAD, HEAD), HEAD)
                src = source.at[0, :, columns]
                if shift == 0:
                    pltpu.make_async_copy(src, land.at[item, 0], a_recv.at[step, pair]).start()
                else:
                    remote(src, land.at[item, shift], a_send.at[step, pair], a_recv.at[step, pair], at_y(shift)).start()

    def heads_wait(step, pair):
        await_bytes(landing(step, pair), a_recv.at[step, pair])

    def heads_sent(step, pair):
        if pair == QUERIES:
            await_bytes(qb.at[step, :, pl.ds(1, 3)], a_send.at[step, pair])
        else:
            await_bytes(kvb.at[step, 0, 0, pl.ds(2 * pair, 2), pl.ds(1, 3)], a_send.at[step, pair])

    def quarter(step, pair, rz, rc):
        return kvb.at[step, rz, rc, pl.ds(2 * pair, 2)]

    def z_copy(half, hop, way):
        step, pair = half // 2, half % 2
        src = kvb.at[step, 0, 0, 2 * pair + way] if hop == 1 else relay.at[half, hop - 2, way]
        dst = kvb.at[step, 1, 0, 2 * pair + way] if hop == 4 else relay.at[half, hop - 1, way]
        return remote(
            src, dst, z_send.at[half, hop - 1, way], z_recv.at[half, hop - 1, way], at_z(1 - 2 * way)
        )

    def z_copies(half, hop):
        return [z_copy(half, hop, way) for way in range(2)]

    def core_copy(step, pair, rz):
        half = 2 * step + pair
        return remote(
            quarter(step, pair, rz, 0), quarter(step, pair, rz, 1),
            c_send.at[half, rz], c_recv.at[half, rz], other_core,
        )

    def z_own(half):
        if half < 2 * STEPS:
            step, pair = half // 2, half % 2
            heads_wait(step, pair)
            start(z_copies(half, 1))
            core_copy(step, pair, 0).start()

    def z_forward(half, hop):
        if 0 <= half < 2 * STEPS:
            recv(z_copies(half, hop))
            start(z_copies(half, hop + 1))

    def w_block(shift, rows):
        there = lax.rem(z + shift + 8, 8)
        return wt.at[lax.div(there, 4) * 2 + core, y, lax.rem(there, 4), x, rows]

    def wz_copy(ring, side):
        rows = pl.ds(0, 80)
        if ring == 3:
            rows = pl.ds(0, 48) if side == 1 else pl.ds(48, 32)
        dst = w_block(-side * ring, rows)
        way = (side + 1) // 2
        src = w_in if ring == 0 else dst
        return remote(src, dst, wz_send.at[ring, way], wz_recv.at[ring, way], at_z(side))

    def group(rel_zh):
        return lax.rem(zh + rel_zh, 2) * 2 + core

    first, rest = pl.ds(0, 3), 3

    def wy_copy(rel_zh, ring, side):
        way = (side + 1) // 2
        there = y if ring == 0 else lax.rem(y - side + 4, 4)
        src = wt.at[group(rel_zh), there, first, x]
        return remote(src, src, wy_send.at[rel_zh, ring, way], wy_recv.at[rel_zh, ring, way], at_y(side))

    def xb_copy(rel_zh, ring, side):
        way = (side + 1) // 2
        there = x if ring == 0 else lax.rem(x - side + 4, 4)
        src = wt.at[group(rel_zh), y, rest, there]
        return remote(src, src, xb_send.at[rel_zh, ring, way], xb_recv.at[rel_zh, ring, way], at_x(side))

    def yb_copy(rel_zh, ring, side):
        way = (side + 1) // 2
        there = y if ring == 0 else lax.rem(y - side + 4, 4)
        src = wt.at[group(rel_zh), there, rest]
        return remote(src, src, yb_send.at[rel_zh, ring, way], yb_recv.at[rel_zh, ring, way], at_y(side))

    def unit_columns(unit):
        return lax.rem(y + COLUMN_ORDER[unit // 2], 4)

    def wx_copy(unit, ring, side):
        way = (side + 1) // 2
        there = x if ring == 0 else lax.rem(x - side + 4, 4)
        src = wt.at[group(unit % 2), unit_columns(unit), first, there]
        return remote(src, src, wx_send.at[unit, ring, way], wx_recv.at[unit, ring, way], at_x(side))

    def wd_copy(unit):
        src = wt.at[group(unit % 2), unit_columns(unit), first]
        return remote(src, src, wd_send.at[unit], wd_recv.at[unit], other_core)

    def db_copy(unit):
        src = wt.at[group(unit % 2), unit_columns(unit), rest]
        return remote(src, src, db_send.at[unit], db_recv.at[unit], other_core)

    def both(make, *key):
        return [make(*key, side) for side in (1, -1)]

    def ring_of(make, index, ring):
        if ring == 0:
            return both(make, index, 0)
        return [make(index, 1, 1 if index % 2 == 0 else -1)]

    def start(copies):
        for copy in copies:
            copy.start()

    def recv(copies):
        for copy in copies:
            copy.wait_recv()

    def recv_other_core(unit):
        other_group = lax.rem(zh + unit % 2, 2) * 2 + 1 - core
        await_bytes(wt.at[other_group, unit_columns(unit), first], wd_recv.at[unit])

    def recv_other_rest(unit):
        other_group = lax.rem(zh + unit % 2, 2) * 2 + 1 - core
        await_bytes(wt.at[other_group, unit_columns(unit), rest], db_recv.at[unit])

    def weigh(step, index):
        rows = pl.ds(index * 2, 2)
        query = qb[step, 0, rows].reshape(2 * TOK, HEAD)
        query_tan = qb[step, 1, rows].reshape(2 * TOK, HEAD)
        key, key_tan = (kvb[step, :, :, item].reshape(16 * TOK, HEAD) for item in range(2))
        scores = lax.dot_general(query, key, NT, preferred_element_type=jnp.float32)
        top = jnp.max(scores, axis=1, keepdims=True)
        weights = jnp.exp2((scores - top) * (SCALE * LOG2E))
        score_tan = lax.dot_general(
            jnp.concatenate([query_tan, query], axis=1),
            jnp.concatenate([key, key_tan], axis=1),
            NT, preferred_element_type=jnp.float32,
        )
        moved = weights * score_tan
        total_ref[index] = jnp.sum(weights, axis=1, keepdims=True)
        spread_ref[index] = jnp.sum(moved, axis=1, keepdims=True) * SCALE
        low_ref[index] = weights.astype(jnp.bfloat16)
        moved_ref[index] = moved.astype(jnp.bfloat16)

    def sums_over(step, index, rz, cores):
        keys = pl.ds((2 * rz + cores.start) * 4 * TOK, cores.size * 4 * TOK)
        value, value_tan = (
            kvb[step, rz, cores, item].reshape(cores.size * 4 * TOK, HEAD) for item in range(2, 4)
        )
        both_values = jnp.concatenate([value, value_tan], axis=1)
        sums = jnp.dot(low_ref[index, :, keys], both_values, preferred_element_type=jnp.float32)
        return sums, jnp.dot(moved_ref[index, :, keys], value, preferred_element_type=jnp.float32)

    def attend(step, index, parts):
        sums, moved = parts[0]
        for more, more_moved in parts[1:]:
            sums, moved = sums + more, moved + more_moved
        rows = pl.ds(index * 2, 2)
        total = total_ref[index]
        plain = sums[:, :HEAD]
        carried = sums[:, HEAD:] + SCALE * moved
        attended = plain / total
        attended_tan = (carried - (spread_ref[index] / total) * plain) / total
        ob[step, rows, 0] = attended.astype(jnp.bfloat16).reshape(2, TOK, HEAD)
        ob[step, rows, 1] = attended_tan.astype(jnp.bfloat16).reshape(2, TOK, HEAD)
        start([home_copy(step, shift) for shift in ((2, 3) if index == 1 else (1,))])

    def home_copy(step, shift):
        return remote(ob.at[step, shift], ab.at[step, shift], r_send.at[step], r_recv.at[step], at_y(-shift))

    def home_wait(step):
        await_bytes(ab.at[step, pl.ds(1, 3)], r_recv.at[step])

    def product(block, step):
        left = [ob[step, 0]] + [ab[step, shift] for shift in range(1, 4)]
        left = jnp.concatenate([item.reshape(2 * TOK, HEAD) for item in left], axis=1)
        lanes = pl.ds(pl.multiple_of(step * HEAD, HEAD), HEAD)
        right = jnp.concatenate(
            [wt[lax.rem(y + shift, 4), block, :, :, :, lanes].reshape(1280, HEAD) for shift in range(4)], axis=1
        )
        return lax.dot_general(left, right, NT, preferred_element_type=jnp.float32)

    def project(first, blocks, start_step, steps):
        def one(index, carry):
            rel = first + lax.div(index, steps)
            step = start_step + lax.rem(index, steps)
            shift = rel + lax.div(rel, 2) * (5 - 2 * rel)
            block = lax.rem(y + shift, 4)
            acc[block] += product(block, step)
            return carry

        lax.fori_loop(0, blocks * steps, one, 0)

    def out_copies(block):
        columns = pl.ds(pl.multiple_of(block * 1280, 1280), 1280)
        return [
            pltpu.make_async_copy(stage.at[block, pl.ds(item * TOK, TOK)], ref.at[0, :, columns], o_sem.at[block, item])
            for item, ref in enumerate((out, out_t))
        ]

    def sends_done():
        for step in range(STEPS):
            for kind in range(3):
                heads_sent(step, kind)
            if step < 3:
                await_bytes(ob.at[step, pl.ds(1, 3)], r_send.at[step])
        copies = []
        for unit in range(8):
            for ring in range(2):
                copies += ring_of(wx_copy, unit, ring)
            copies += [wd_copy(unit), db_copy(unit)]
        for ring in range(4):
            copies += both(wz_copy, ring)
        for rel_zh in range(2):
            for ring in range(2):
                for make in (wy_copy, xb_copy, yb_copy):
                    copies += ring_of(make, rel_zh, ring)
        for half in range(2 * STEPS):
            copies.append(core_copy(half // 2, half % 2, 0))
            for hop in range(1, 5):
                if half + hop < 12:
                    copies += z_copies(half, hop)
            if half < 8:
                copies.append(core_copy(half // 2, half % 2, 1))
        for copy in copies:
            copy.wait_send()

    def x_forward(unit):
        recv(ring_of(wx_copy, unit, 0))
        start(ring_of(wx_copy, unit, 1))
        if 2 <= unit + 2 <= 7:
            start(ring_of(wx_copy, unit + 2, 0))

    def x_done(unit):
        recv(ring_of(wx_copy, unit, 1))
        wd_copy(unit).start()

    def z_arrived(half):
        if 0 <= half:
            recv(z_copies(half, 4))
            core_copy(half // 2, half % 2, 1).start()

    def pair_here(half):
        step, pair = half // 2, half % 2
        core_copy(step, pair, 0).wait_recv()
        core_copy(step, pair, 1).wait_recv()
        if pair == KEYS:
            heads_wait(step, QUERIES)

    everywhere = pl.ds(0, 2)

    def work(half, index):
        if half < 0:
            return
        step = half // 2
        if half % 2 == KEYS:
            weigh(step, index)
        else:
            attend(step, index, [sums_over(step, index, rz, everywhere) for rz in range(2)])

    def turn(at, after_first=(), after_second=(), after_last=()):
        z_own(at)
        z_forward(at - 3, 3)
        z_arrived(at - 4)
        for call in after_first:
            call()
        z_forward(at - 2, 2)
        if at >= 4:
            pair_here(at - 4)
        work(at - 4, 1)
        for call in after_second:
            call()
        z_forward(at - 1, 1)
        work(at - 4, 0)
        for call in after_last:
            call()

    def y_ring(make, ring):
        for rel_zh in range(2):
            start(ring_of(make, rel_zh, ring))

    def y_recv(make, ring):
        for rel_zh in range(2):
            recv(ring_of(make, rel_zh, ring))

    def do(call, *args):
        return lambda: call(*args)

    def wz_ring(ring):
        recv(both(wz_copy, ring - 1))
        start(both(wz_copy, ring))

    def weights_first():
        recv(both(wz_copy, 3))
        load_w.wait()
        start(ring_of(wx_copy, 0, 0))
        y_ring(wy_copy, 0)
        y_ring(xb_copy, 0)
        start(ring_of(wx_copy, 1, 0))

    def rest_to_core(*units):
        for unit in units:
            db_copy(unit).start()

    def from_core(*units):
        for unit in units:
            recv_other_core(unit)
            recv_other_rest(unit)

    def heads_more(*wanted):
        for step, pair in wanted:
            heads_start(step, pair)

    heads_start(0, KEYS)
    start(both(wz_copy, 0))
    heads_start(0, VALUES)
    acc[...] = jnp.zeros_like(acc)
    wz_ring(1)
    turn(0)
    heads_start(1, KEYS)
    wz_ring(2)
    turn(1)
    heads_start(1, VALUES)
    wz_ring(3)
    turn(2)
    heads_start(0, QUERIES)
    weights_first()
    heads_start(2, KEYS)
    turn(3, [do(heads_start, 2, VALUES)], [], [do(y_recv, wy_copy, 0), do(x_forward, 0)])
    turn(
        4,
        [do(y_ring, wy_copy, 1), do(heads_more, (3, KEYS), (3, VALUES), (1, QUERIES)), do(y_recv, xb_copy, 0)],
        [do(y_ring, xb_copy, 1), do(x_forward, 1)],
        [do(x_done, 0)],
    )
    turn(
        5,
        [do(heads_more, (4, KEYS), (4, VALUES), (2, QUERIES))],
        [do(x_forward, 2), do(x_done, 1)],
        [do(y_recv, xb_copy, 1), do(y_recv, wy_copy, 1), do(rest_to_core, 0, 1), do(y_ring, yb_copy, 0)],
    )
    turn(6, [do(heads_more, (3, QUERIES), (4, QUERIES))], [do(x_forward, 3), do(x_done, 2)], [do(x_forward, 4)])
    turn(7, [do(x_done, 3)], [do(x_done, 4)], [do(x_forward, 5)])
    turn(
        8,
        [do(y_recv, yb_copy, 0), do(y_ring, yb_copy, 1)],
        [do(rest_to_core, 2, 3, 4, 5), do(x_done, 5)],
        [do(x_forward, 6)],
    )
    turn(
        9,
        [do(x_done, 6)],
        [do(from_core, 0, 1, 2, 3, 4, 5)],
        [do(x_forward, 7), do(home_wait, 0), do(project, 0, 3, 0, 1)],
    )
    turn(
        10,
        [do(y_recv, yb_copy, 1), do(rest_to_core, 6, 7), do(x_done, 7)],
        [do(home_wait, 1)],
        [do(project, 0, 3, 1, 1)],
    )
    turn(11, [do(from_core, 6, 7)], [do(home_wait, 2)], [do(project, 0, 4, 2, 1), do(project, 3, 1, 0, 2)])
    turn(12, [do(sends_done)], [], [do(home_wait, 3), do(project, 0, 4, 3, 1)])
    last = STEPS - 1
    core_copy(last, VALUES, 0).wait_recv()
    for index in range(2):
        sums_ref[index], carry_ref[index] = sums_over(last, index, 0, everywhere)
    z_arrived(9)
    for index in range(2):
        sums, moved = sums_over(last, index, 1, pl.ds(0, 1))
        sums_ref[index] += sums
        carry_ref[index] += moved
    core_copy(last, VALUES, 1).wait_recv()
    for index in (1, 0):
        attend(last, index, [(sums_ref[index], carry_ref[index]), sums_over(last, index, 1, pl.ds(1, 1))])

    home_wait(last)

    def finish(block, carry):
        stage[block] = (acc[block] + product(block, last)).astype(jnp.bfloat16)
        start(out_copies(block))
        return carry

    lax.fori_loop(0, 4, finish, 0)
    for half, hop in ((8, 4), (9, 3), (9, 4)):
        for copy in z_copies(half, hop):
            copy.wait_send()
    core_copy(last, KEYS, 1).wait_send()
    core_copy(last, VALUES, 1).wait_send()
    for step in (last - 1, last):
        await_bytes(ob.at[step, pl.ds(1, 3)], r_send.at[step])

    def drain(block, carry):
        for copy in out_copies(block):
            copy.wait()
        return carry

    lax.fori_loop(0, 4, drain, 0)


def per_device(*arrays):
    dma = pltpu.SemaphoreType.DMA
    low = jnp.bfloat16
    result = jax.ShapeDtypeStruct((1, TOK, 5120), low)
    anywhere = pl.BlockSpec(memory_space=pl.ANY)
    return pl.pallas_call(
        kernel,
        out_shape=(result, result),
        in_specs=[anywhere] * 7,
        out_specs=(anywhere, anywhere),
        scratch_shapes=[
            pltpu.VMEM((2 * STEPS, 3, 2, 4, TOK, HEAD), low),
            pltpu.VMEM((STEPS, 2, 2, 4, 4, TOK, HEAD), low),
            pltpu.VMEM((STEPS, 2, 4, TOK, HEAD), low),
            pltpu.VMEM((STEPS, 4, 2, TOK, HEAD), low),
            pltpu.VMEM((STEPS, 4, 2, TOK, HEAD), low),
            pltpu.VMEM((4, 4, 4, 4, 80, 640), low),
            pltpu.VMEM((4, 2 * TOK, 1280), jnp.float32),
            pltpu.VMEM((4, 2 * TOK, 1280), low),
            pltpu.VMEM((2, 2 * TOK, 16 * TOK), low),
            pltpu.VMEM((2, 2 * TOK, 16 * TOK), low),
            pltpu.VMEM((2, 2 * TOK, 1), jnp.float32),
            pltpu.VMEM((2, 2 * TOK, 1), jnp.float32),
            pltpu.VMEM((2, 2 * TOK, 2 * HEAD), jnp.float32),
            pltpu.VMEM((2, 2 * TOK, HEAD), jnp.float32),
            dma((STEPS, 3)), dma((STEPS, 3)),
            dma((2 * STEPS, 4, 2)), dma((2 * STEPS, 4, 2)),
            dma((2 * STEPS, 2)), dma((2 * STEPS, 2)),
            dma((STEPS,)), dma((STEPS,)),
            dma((4, 2)), dma((4, 2)),
            dma((2, 2, 2)), dma((2, 2, 2)),
            dma((8, 2, 2)), dma((8, 2, 2)),
            dma((8,)), dma((8,)),
            dma((2, 2, 2)), dma((2, 2, 2)),
            dma((2, 2, 2)), dma((2, 2, 2)),
            dma((8,)), dma((8,)),
            dma, dma((4, 2)),
        ],
        compiler_params=pltpu.CompilerParams(
            collective_id=0, has_side_effects=True, vmem_limit_bytes=64 * 1024 * 1024
        ),
    )(*arrays[:6], arrays[6].T)


def solution(mesh):
    rows = P("dp", ("uly", "blk"), None)
    return jax.shard_map(
        per_device,
        mesh=mesh,
        in_specs=(rows,) * 6 + (P("uly", ("blk", "dp")),),
        out_specs=(rows, rows),
        check_vma=False,
    )
```

```python
import jax
import jax.numpy as jnp
from jax import lax
from jax.experimental import pallas as pl
from jax.experimental.pallas import tpu as pltpu
from jax.sharding import PartitionSpec as P

HEAD = 128
STEPS = 5
TOK = 128
SCALE = HEAD ** -0.5
LOG2E = 1.4426950408889634
MESH_IDS = pl.DeviceIdType.MESH
NT = (((1,), (1,)), ((), ()))
KEYS, VALUES, QUERIES = 0, 1, 2
COLUMN_ORDER = (0, 1, 3, 2)


def kernel(
    q_in, k_in, v_in, qt_in, kt_in, vt_in, w_in, out, out_t, relay,
    kvb, qb, ob, ab, wt, acc, low_ref, moved_ref, total_ref, spread_ref, sums_ref, carry_ref,
    a_send, a_recv, z_send, z_recv, c_send, c_recv, r_send, r_recv,
    wz_send, wz_recv, wy_send, wy_recv, wx_send, wx_recv, wd_send, wd_recv,
    xb_send, xb_recv, yb_send, yb_recv, db_send, db_recv,
    l_sem,
):
    dp = lax.axis_index("dp")
    uly = lax.axis_index("uly")
    y = lax.axis_index("blk")
    x = lax.rem(dp, 4)
    zl = lax.div(dp, 4)
    zh = lax.div(uly, 2)
    core = lax.rem(uly, 2)
    z = zh * 4 + zl

    def at_z(shift):
        there = lax.rem(z + shift + 8, 8)
        return {
            "dp": lax.rem(there, 4) * 4 + x,
            "uly": lax.div(there, 4) * 2 + core,
            "blk": y,
        }

    def at_y(shift):
        return {"dp": dp, "uly": uly, "blk": lax.rem(y + shift + 4, 4)}

    def at_x(shift):
        return {"dp": zl * 4 + lax.rem(x + shift + 4, 4), "uly": uly, "blk": y}

    other_core = {"dp": dp, "uly": zh * 2 + 1 - core, "blk": y}

    def remote(src, dst, send, recv, where):
        return pltpu.make_async_remote_copy(
            src_ref=src, dst_ref=dst, send_sem=send, recv_sem=recv,
            device_id=where, device_id_type=MESH_IDS,
        )

    def await_bytes(ref, sem):
        pltpu.make_async_copy(ref, ref, sem).wait()

    load_w = pltpu.make_async_copy(w_in, wt.at[uly, y, zl, x], l_sem)
    load_w.start()

    partners = [at_y(1), at_y(2), at_y(3), at_x(1), at_x(-1), at_z(1), at_z(-1), other_core]
    barrier = pltpu.get_barrier_semaphore()
    for where in partners:
        pl.semaphore_signal(barrier, inc=1, device_id=where, device_id_type=MESH_IDS)
    pl.semaphore_wait(barrier, len(partners))

    pairs = ((k_in, kt_in), (v_in, vt_in), (q_in, qt_in))

    def landing(step, pair):
        if pair == QUERIES:
            return qb.at[step]
        return kvb.at[step, 0, 0, pl.ds(2 * pair, 2)]

    def heads_start(step, pair):
        land = landing(step, pair)
        for item in range(2):
            source = pairs[pair][item]
            for shift in (2, 1, 3, 0):
                owner = lax.rem(y + shift, 4)
                columns = pl.ds(pl.multiple_of(owner * (STEPS * HEAD) + step * HEAD, HEAD), HEAD)
                src = source.at[0, :, columns]
                if shift == 0:
                    pltpu.make_async_copy(src, land.at[item, 0], a_recv.at[step, pair]).start()
                else:
                    remote(src, land.at[item, shift], a_send.at[step, pair], a_recv.at[step, pair], at_y(shift)).start()

    def heads_wait(step, pair):
        await_bytes(landing(step, pair), a_recv.at[step, pair])

    def heads_sent(step, pair):
        if pair == QUERIES:
            await_bytes(qb.at[step, :, pl.ds(1, 3)], a_send.at[step, pair])
        else:
            await_bytes(kvb.at[step, 0, 0, pl.ds(2 * pair, 2), pl.ds(1, 3)], a_send.at[step, pair])

    def quarter(step, pair, rz, rc):
        return kvb.at[step, rz, rc, pl.ds(2 * pair, 2)]

    def z_copy(half, hop, way):
        step, pair = half // 2, half % 2
        src = kvb.at[step, 0, 0, 2 * pair + way] if hop == 1 else relay.at[half, hop - 2, way]
        dst = kvb.at[step, 1, 0, 2 * pair + way] if hop == 4 else relay.at[half, hop - 1, way]
        return remote(
            src, dst, z_send.at[half, hop - 1, way], z_recv.at[half, hop - 1, way], at_z(1 - 2 * way)
        )

    def z_copies(half, hop):
        return [z_copy(half, hop, way) for way in range(2)]

    def core_copy(step, pair, rz):
        half = 2 * step + pair
        return remote(
            quarter(step, pair, rz, 0), quarter(step, pair, rz, 1),
            c_send.at[half, rz], c_recv.at[half, rz], other_core,
        )

    def z_own(half):
        if half < 2 * STEPS:
            step, pair = half // 2, half % 2
            heads_wait(step, pair)
            start(z_copies(half, 1))
            core_copy(step, pair, 0).start()

    def z_forward(half, hop):
        if 0 <= half < 2 * STEPS:
            recv(z_copies(half, hop))
            start(z_copies(half, hop + 1))

    def w_block(shift, rows):
        there = lax.rem(z + shift + 8, 8)
        return wt.at[lax.div(there, 4) * 2 + core, y, lax.rem(there, 4), x, rows]

    def wz_copy(ring, side):
        rows = pl.ds(0, 80)
        if ring == 3:
            rows = pl.ds(0, 48) if side == 1 else pl.ds(48, 32)
        dst = w_block(-side * ring, rows)
        way = (side + 1) // 2
        src = w_in if ring == 0 else dst
        return remote(src, dst, wz_send.at[ring, way], wz_recv.at[ring, way], at_z(side))

    def group(rel_zh):
        return lax.rem(zh + rel_zh, 2) * 2 + core

    first, rest = pl.ds(0, 3), 3

    def wy_copy(rel_zh, ring, side):
        way = (side + 1) // 2
        there = y if ring == 0 else lax.rem(y - side + 4, 4)
        src = wt.at[group(rel_zh), there, first, x]
        return remote(src, src, wy_send.at[rel_zh, ring, way], wy_recv.at[rel_zh, ring, way], at_y(side))

    def xb_copy(rel_zh, ring, side):
        way = (side + 1) // 2
        there = x if ring == 0 else lax.rem(x - side + 4, 4)
        src = wt.at[group(rel_zh), y, rest, there]
        return remote(src, src, xb_send.at[rel_zh, ring, way], xb_recv.at[rel_zh, ring, way], at_x(side))

    def yb_copy(rel_zh, ring, side):
        way = (side + 1) // 2
        there = y if ring == 0 else lax.rem(y - side + 4, 4)
        src = wt.at[group(rel_zh), there, rest]
        return remote(src, src, yb_send.at[rel_zh, ring, way], yb_recv.at[rel_zh, ring, way], at_y(side))

    def unit_columns(unit):
        return lax.rem(y + COLUMN_ORDER[unit // 2], 4)

    def wx_copy(unit, ring, side):
        way = (side + 1) // 2
        there = x if ring == 0 else lax.rem(x - side + 4, 4)
        src = wt.at[group(unit % 2), unit_columns(unit), first, there]
        return remote(src, src, wx_send.at[unit, ring, way], wx_recv.at[unit, ring, way], at_x(side))

    def wd_copy(unit):
        src = wt.at[group(unit % 2), unit_columns(unit), first]
        return remote(src, src, wd_send.at[unit], wd_recv.at[unit], other_core)

    def db_copy(unit):
        src = wt.at[group(unit % 2), unit_columns(unit), rest]
        return remote(src, src, db_send.at[unit], db_recv.at[unit], other_core)

    def both(make, *key):
        return [make(*key, side) for side in (1, -1)]

    def ring_of(make, index, ring):
        if ring == 0:
            return both(make, index, 0)
        return [make(index, 1, 1 if index % 2 == 0 else -1)]

    def start(copies):
        for copy in copies:
            copy.start()

    def recv(copies):
        for copy in copies:
            copy.wait_recv()

    def recv_other_core(unit):
        other_group = lax.rem(zh + unit % 2, 2) * 2 + 1 - core
        await_bytes(wt.at[other_group, unit_columns(unit), first], wd_recv.at[unit])

    def recv_other_rest(unit):
        other_group = lax.rem(zh + unit % 2, 2) * 2 + 1 - core
        await_bytes(wt.at[other_group, unit_columns(unit), rest], db_recv.at[unit])

    def weigh(step, index):
        rows = pl.ds(index * 2, 2)
        query = qb[step, 0, rows].reshape(2 * TOK, HEAD)
        query_tan = qb[step, 1, rows].reshape(2 * TOK, HEAD)
        key, key_tan = (kvb[step, :, :, item].reshape(16 * TOK, HEAD) for item in range(2))
        scores = lax.dot_general(query, key, NT, preferred_element_type=jnp.float32)
        top = jnp.max(scores, axis=1, keepdims=True)
        weights = jnp.exp2((scores - top) * (SCALE * LOG2E))
        score_tan = lax.dot_general(
            jnp.concatenate([query_tan, query], axis=1),
            jnp.concatenate([key, key_tan], axis=1),
            NT, preferred_element_type=jnp.float32,
        )
        moved = weights * score_tan
        total_ref[index] = jnp.sum(weights, axis=1, keepdims=True)
        spread_ref[index] = jnp.sum(moved, axis=1, keepdims=True) * SCALE
        low_ref[index] = weights.astype(jnp.bfloat16)
        moved_ref[index] = moved.astype(jnp.bfloat16)

    def sums_over(step, index, rz, cores):
        keys = pl.ds((2 * rz + cores.start) * 4 * TOK, cores.size * 4 * TOK)
        value, value_tan = (
            kvb[step, rz, cores, item].reshape(cores.size * 4 * TOK, HEAD) for item in range(2, 4)
        )
        both_values = jnp.concatenate([value, value_tan], axis=1)
        sums = jnp.dot(low_ref[index, :, keys], both_values, preferred_element_type=jnp.float32)
        return sums, jnp.dot(moved_ref[index, :, keys], value, preferred_element_type=jnp.float32)

    def attend(step, index, parts):
        sums, moved = parts[0]
        for more, more_moved in parts[1:]:
            sums, moved = sums + more, moved + more_moved
        rows = pl.ds(index * 2, 2)
        total = total_ref[index]
        plain = sums[:, :HEAD]
        carried = sums[:, HEAD:] + SCALE * moved
        attended = plain / total
        attended_tan = (carried - (spread_ref[index] / total) * plain) / total
        ob[step, rows, 0] = attended.astype(jnp.bfloat16).reshape(2, TOK, HEAD)
        ob[step, rows, 1] = attended_tan.astype(jnp.bfloat16).reshape(2, TOK, HEAD)
        start([home_copy(step, shift) for shift in ((2, 3) if index == 1 else (1,))])

    def home_copy(step, shift):
        return remote(ob.at[step, shift], ab.at[step, shift], r_send.at[step], r_recv.at[step], at_y(-shift))

    def home_wait(step):
        await_bytes(ab.at[step, pl.ds(1, 3)], r_recv.at[step])

    def product(block, step):
        left = [ob[step, 0]] + [ab[step, shift] for shift in range(1, 4)]
        left = jnp.concatenate([item.reshape(2 * TOK, HEAD) for item in left], axis=1)
        lanes = pl.ds(pl.multiple_of(step * HEAD, HEAD), HEAD)
        right = jnp.concatenate(
            [wt[lax.rem(y + shift, 4), block, :, :, :, lanes].reshape(1280, HEAD) for shift in range(4)], axis=1
        )
        return lax.dot_general(left, right, NT, preferred_element_type=jnp.float32)

    def project(first, blocks, start_step, steps):
        def one(index, carry):
            rel = first + lax.div(index, steps)
            step = start_step + lax.rem(index, steps)
            shift = rel + lax.div(rel, 2) * (5 - 2 * rel)
            block = lax.rem(y + shift, 4)
            acc[block] += product(block, step)
            return carry

        lax.fori_loop(0, blocks * steps, one, 0)

    def sends_done():
        for step in range(STEPS):
            for kind in range(3):
                heads_sent(step, kind)
            if step < 3:
                await_bytes(ob.at[step, pl.ds(1, 3)], r_send.at[step])
        copies = []
        for unit in range(8):
            for ring in range(2):
                copies += ring_of(wx_copy, unit, ring)
            copies += [wd_copy(unit), db_copy(unit)]
        for ring in range(4):
            copies += both(wz_copy, ring)
        for rel_zh in range(2):
            for ring in range(2):
                for make in (wy_copy, xb_copy, yb_copy):
                    copies += ring_of(make, rel_zh, ring)
        for half in range(2 * STEPS):
            copies.append(core_copy(half // 2, half % 2, 0))
            for hop in range(1, 5):
                if half + hop < 12:
                    copies += z_copies(half, hop)
            if half < 8:
                copies.append(core_copy(half // 2, half % 2, 1))
        for copy in copies:
            copy.wait_send()

    def x_forward(unit):
        recv(ring_of(wx_copy, unit, 0))
        start(ring_of(wx_copy, unit, 1))
        if 2 <= unit + 2 <= 7:
            start(ring_of(wx_copy, unit + 2, 0))

    def x_done(unit):
        recv(ring_of(wx_copy, unit, 1))
        wd_copy(unit).start()

    def z_arrived(half):
        if 0 <= half:
            recv(z_copies(half, 4))
            core_copy(half // 2, half % 2, 1).start()

    def pair_here(half):
        step, pair = half // 2, half % 2
        core_copy(step, pair, 0).wait_recv()
        core_copy(step, pair, 1).wait_recv()
        if pair == KEYS:
            heads_wait(step, QUERIES)

    everywhere = pl.ds(0, 2)

    def work(half, index):
        if half < 0:
            return
        step = half // 2
        if half % 2 == KEYS:
            weigh(step, index)
        else:
            attend(step, index, [sums_over(step, index, rz, everywhere) for rz in range(2)])

    def turn(at, after_first=(), after_second=(), after_last=()):
        z_own(at)
        z_forward(at - 3, 3)
        z_arrived(at - 4)
        for call in after_first:
            call()
        z_forward(at - 2, 2)
        if at >= 4:
            pair_here(at - 4)
        work(at - 4, 1)
        for call in after_second:
            call()
        z_forward(at - 1, 1)
        work(at - 4, 0)
        for call in after_last:
            call()

    def y_ring(make, ring):
        for rel_zh in range(2):
            start(ring_of(make, rel_zh, ring))

    def y_recv(make, ring):
        for rel_zh in range(2):
            recv(ring_of(make, rel_zh, ring))

    def do(call, *args):
        return lambda: call(*args)

    def wz_ring(ring):
        recv(both(wz_copy, ring - 1))
        start(both(wz_copy, ring))

    def weights_first():
        recv(both(wz_copy, 3))
        load_w.wait()
        start(ring_of(wx_copy, 0, 0))
        y_ring(wy_copy, 0)
        y_ring(xb_copy, 0)
        start(ring_of(wx_copy, 1, 0))

    def rest_to_core(*units):
        for unit in units:
            db_copy(unit).start()

    def from_core(*units):
        for unit in units:
            recv_other_core(unit)
            recv_other_rest(unit)

    def heads_more(*wanted):
        for step, pair in wanted:
            heads_start(step, pair)

    heads_start(0, KEYS)
    start(both(wz_copy, 0))
    heads_start(0, VALUES)
    acc[...] = jnp.zeros_like(acc)
    wz_ring(1)
    turn(0)
    heads_start(1, KEYS)
    wz_ring(2)
    turn(1)
    heads_start(1, VALUES)
    wz_ring(3)
    turn(2)
    heads_start(0, QUERIES)
    weights_first()
    heads_start(2, KEYS)
    turn(3, [do(heads_start, 2, VALUES)], [], [do(y_recv, wy_copy, 0), do(x_forward, 0)])
    turn(
        4,
        [do(y_ring, wy_copy, 1), do(heads_more, (3, KEYS), (3, VALUES), (1, QUERIES)), do(y_recv, xb_copy, 0)],
        [do(y_ring, xb_copy, 1), do(x_forward, 1)],
        [do(x_done, 0)],
    )
    turn(
        5,
        [do(heads_more, (4, KEYS), (4, VALUES), (2, QUERIES))],
        [do(x_forward, 2), do(x_done, 1)],
        [do(y_recv, xb_copy, 1), do(y_recv, wy_copy, 1), do(rest_to_core, 0, 1), do(y_ring, yb_copy, 0)],
    )
    turn(6, [do(heads_more, (3, QUERIES), (4, QUERIES))], [do(x_forward, 3), do(x_done, 2)], [do(x_forward, 4)])
    turn(7, [do(x_done, 3)], [do(x_done, 4)], [do(x_forward, 5)])
    turn(
        8,
        [do(y_recv, yb_copy, 0), do(y_ring, yb_copy, 1)],
        [do(rest_to_core, 2, 3, 4, 5), do(x_done, 5)],
        [do(x_forward, 6)],
    )
    turn(
        9,
        [do(x_done, 6)],
        [do(from_core, 0, 1, 2, 3, 4, 5)],
        [do(x_forward, 7), do(home_wait, 0), do(project, 0, 3, 0, 1)],
    )
    turn(
        10,
        [do(y_recv, yb_copy, 1), do(rest_to_core, 6, 7), do(x_done, 7)],
        [do(home_wait, 1)],
        [do(project, 0, 3, 1, 1)],
    )
    turn(11, [], [do(home_wait, 2)], [do(project, 0, 3, 2, 1)])
    turn(12)
    last = STEPS - 1
    core_copy(last, VALUES, 0).wait_recv()
    for index in range(2):
        sums_ref[index], carry_ref[index] = sums_over(last, index, 0, everywhere)
    z_arrived(9)
    for index in range(2):
        sums, moved = sums_over(last, index, 1, pl.ds(0, 1))
        sums_ref[index] += sums
        carry_ref[index] += moved
    core_copy(last, VALUES, 1).wait_recv()
    for index in (1, 0):
        attend(last, index, [(sums_ref[index], carry_ref[index]), sums_over(last, index, 1, pl.ds(1, 1))])
    from_core(6, 7)
    project(3, 1, 0, 3)
    home_wait(last - 1)
    project(0, 4, last - 1, 1)
    sends_done()

    home_wait(last)

    def finish(block, carry):
        columns = pl.ds(pl.multiple_of(block * 1280, 1280), 1280)
        sums = (acc[block] + product(block, last)).astype(jnp.bfloat16)
        out[0, :, columns] = sums[:TOK]
        out_t[0, :, columns] = sums[TOK:]
        return carry

    lax.fori_loop(0, 4, finish, 0)
    for half, hop in ((8, 4), (9, 3), (9, 4)):
        for copy in z_copies(half, hop):
            copy.wait_send()
    core_copy(last, KEYS, 1).wait_send()
    core_copy(last, VALUES, 1).wait_send()
    for step in (last - 1, last):
        await_bytes(ob.at[step, pl.ds(1, 3)], r_send.at[step])


def per_device(*arrays):
    dma = pltpu.SemaphoreType.DMA
    low = jnp.bfloat16
    result = pltpu.VMEM((1, TOK, 5120), low)
    anywhere = pl.BlockSpec(memory_space=pl.ANY)
    return pl.pallas_call(
        kernel,
        out_shape=(result, result, jax.ShapeDtypeStruct((2 * STEPS, 3, 2, 4, TOK, HEAD), low)),
        in_specs=[anywhere] * 7,
        out_specs=(pl.BlockSpec(memory_space=pltpu.VMEM),) * 2 + (anywhere,),
        scratch_shapes=[
            pltpu.VMEM((STEPS, 2, 2, 4, 4, TOK, HEAD), low),
            pltpu.VMEM((STEPS, 2, 4, TOK, HEAD), low),
            pltpu.VMEM((STEPS, 4, 2, TOK, HEAD), low),
            pltpu.VMEM((STEPS, 4, 2, TOK, HEAD), low),
            pltpu.VMEM((4, 4, 4, 4, 80, 640), low),
            pltpu.VMEM((4, 2 * TOK, 1280), jnp.float32),
            pltpu.VMEM((2, 2 * TOK, 16 * TOK), low),
            pltpu.VMEM((2, 2 * TOK, 16 * TOK), low),
            pltpu.VMEM((2, 2 * TOK, 1), jnp.float32),
            pltpu.VMEM((2, 2 * TOK, 1), jnp.float32),
            pltpu.VMEM((2, 2 * TOK, 2 * HEAD), jnp.float32),
            pltpu.VMEM((2, 2 * TOK, HEAD), jnp.float32),
            dma((STEPS, 3)), dma((STEPS, 3)),
            dma((2 * STEPS, 4, 2)), dma((2 * STEPS, 4, 2)),
            dma((2 * STEPS, 2)), dma((2 * STEPS, 2)),
            dma((STEPS,)), dma((STEPS,)),
            dma((4, 2)), dma((4, 2)),
            dma((2, 2, 2)), dma((2, 2, 2)),
            dma((8, 2, 2)), dma((8, 2, 2)),
            dma((8,)), dma((8,)),
            dma((2, 2, 2)), dma((2, 2, 2)),
            dma((2, 2, 2)), dma((2, 2, 2)),
            dma((8,)), dma((8,)),
            dma,
        ],
        compiler_params=pltpu.CompilerParams(
            collective_id=0, has_side_effects=True, vmem_limit_bytes=60 * 1024 * 1024
        ),
    )(*arrays[:6], arrays[6].T)[:2]


def solution(mesh):
    rows = P("dp", ("uly", "blk"), None)
    return jax.shard_map(
        per_device,
        mesh=mesh,
        in_specs=(rows,) * 6 + (P("uly", ("blk", "dp")),),
        out_specs=(rows, rows),
        check_vma=False,
    )
```

```python
import jax
import jax.numpy as jnp
from jax import lax
from jax.experimental import pallas as pl
from jax.experimental.pallas import tpu as pltpu
from jax.sharding import PartitionSpec as P

HEAD = 128
STEPS = 5
TOK = 128
SCALE = HEAD ** -0.5
LOG2E = 1.4426950408889634
MESH_IDS = pl.DeviceIdType.MESH
NT = (((1,), (1,)), ((), ()))
KEYS, VALUES, QUERIES = 0, 1, 2
COLUMN_ORDER = (0, 1, 3, 2)


def kernel(
    q_in, k_in, v_in, qt_in, kt_in, vt_in, w_in, out, out_t,
    relay, kvb, qb, ob, ab, wt, acc, low_ref, moved_ref, total_ref, spread_ref, sums_ref, carry_ref,
    a_send, a_recv, z_send, z_recv, c_send, c_recv, r_send, r_recv,
    wz_send, wz_recv, wy_send, wy_recv, wx_send, wx_recv, wd_send, wd_recv,
    xb_send, xb_recv, yb_send, yb_recv, db_send, db_recv,
    l_sem,
):
    dp = lax.axis_index("dp")
    uly = lax.axis_index("uly")
    y = lax.axis_index("blk")
    x = lax.rem(dp, 4)
    zl = lax.div(dp, 4)
    zh = lax.div(uly, 2)
    core = lax.rem(uly, 2)
    z = zh * 4 + zl

    def at_z(shift):
        there = lax.rem(z + shift + 8, 8)
        return {
            "dp": lax.rem(there, 4) * 4 + x,
            "uly": lax.div(there, 4) * 2 + core,
            "blk": y,
        }

    def at_y(shift):
        return {"dp": dp, "uly": uly, "blk": lax.rem(y + shift + 4, 4)}

    def at_x(shift):
        return {"dp": zl * 4 + lax.rem(x + shift + 4, 4), "uly": uly, "blk": y}

    other_core = {"dp": dp, "uly": zh * 2 + 1 - core, "blk": y}

    def remote(src, dst, send, recv, where):
        return pltpu.make_async_remote_copy(
            src_ref=src, dst_ref=dst, send_sem=send, recv_sem=recv,
            device_id=where, device_id_type=MESH_IDS,
        )

    def await_bytes(ref, sem):
        pltpu.make_async_copy(ref, ref, sem).wait()

    load_w = pltpu.make_async_copy(w_in, wt.at[uly, y, zl, x], l_sem)
    load_w.start()

    partners = [at_y(1), at_y(2), at_y(3), at_x(1), at_x(-1), at_z(1), at_z(-1), other_core]
    barrier = pltpu.get_barrier_semaphore()
    for where in partners:
        pl.semaphore_signal(barrier, inc=1, device_id=where, device_id_type=MESH_IDS)
    pl.semaphore_wait(barrier, len(partners))

    pairs = ((k_in, kt_in), (v_in, vt_in), (q_in, qt_in))

    def landing(step, pair):
        if pair == QUERIES:
            return qb.at[step]
        return kvb.at[step, 0, 0, pl.ds(2 * pair, 2)]

    def heads_start(step, pair):
        land = landing(step, pair)
        for item in range(2):
            source = pairs[pair][item]
            for shift in (2, 1, 3, 0):
                owner = lax.rem(y + shift, 4)
                columns = pl.ds(pl.multiple_of(owner * (STEPS * HEAD) + step * HEAD, HEAD), HEAD)
                src = source.at[0, :, columns]
                if shift == 0:
                    pltpu.make_async_copy(src, land.at[item, 0], a_recv.at[step, pair]).start()
                else:
                    remote(src, land.at[item, shift], a_send.at[step, pair], a_recv.at[step, pair], at_y(shift)).start()

    def heads_wait(step, pair):
        await_bytes(landing(step, pair), a_recv.at[step, pair])

    def heads_sent(step, pair):
        if pair == QUERIES:
            await_bytes(qb.at[step, :, pl.ds(1, 3)], a_send.at[step, pair])
        else:
            await_bytes(kvb.at[step, 0, 0, pl.ds(2 * pair, 2), pl.ds(1, 3)], a_send.at[step, pair])

    def quarter(step, pair, rz, rc):
        return kvb.at[step, rz, rc, pl.ds(2 * pair, 2)]

    def z_copy(half, hop, way):
        step, pair = half // 2, half % 2
        src = kvb.at[step, 0, 0, 2 * pair + way] if hop == 1 else relay.at[half, hop - 2, way]
        dst = kvb.at[step, 1, 0, 2 * pair + way] if hop == 4 else relay.at[half, hop - 1, way]
        return remote(
            src, dst, z_send.at[half, hop - 1, way], z_recv.at[half, hop - 1, way], at_z(1 - 2 * way)
        )

    def z_copies(half, hop):
        return [z_copy(half, hop, way) for way in range(2)]

    def core_copy(step, pair, rz):
        half = 2 * step + pair
        return remote(
            quarter(step, pair, rz, 0), quarter(step, pair, rz, 1),
            c_send.at[half, rz], c_recv.at[half, rz], other_core,
        )

    def z_own(half):
        if half < 2 * STEPS:
            step, pair = half // 2, half % 2
            heads_wait(step, pair)
            start(z_copies(half, 1))
            core_copy(step, pair, 0).start()

    def z_forward(half, hop):
        if 0 <= half < 2 * STEPS:
            recv(z_copies(half, hop))
            start(z_copies(half, hop + 1))

    def w_block(shift, rows):
        there = lax.rem(z + shift + 8, 8)
        return wt.at[lax.div(there, 4) * 2 + core, y, lax.rem(there, 4), x, rows]

    def wz_copy(ring, side):
        rows = pl.ds(0, 80)
        if ring == 3:
            rows = pl.ds(0, 48) if side == 1 else pl.ds(48, 32)
        dst = w_block(-side * ring, rows)
        way = (side + 1) // 2
        src = w_in if ring == 0 else dst
        return remote(src, dst, wz_send.at[ring, way], wz_recv.at[ring, way], at_z(side))

    def group(rel_zh):
        return lax.rem(zh + rel_zh, 2) * 2 + core

    first, rest = pl.ds(0, 3), 3

    def wy_copy(rel_zh, ring, side):
        way = (side + 1) // 2
        there = y if ring == 0 else lax.rem(y - side + 4, 4)
        src = wt.at[group(rel_zh), there, first, x]
        return remote(src, src, wy_send.at[rel_zh, ring, way], wy_recv.at[rel_zh, ring, way], at_y(side))

    def xb_copy(rel_zh, ring, side):
        way = (side + 1) // 2
        there = x if ring == 0 else lax.rem(x - side + 4, 4)
        src = wt.at[group(rel_zh), y, rest, there]
        return remote(src, src, xb_send.at[rel_zh, ring, way], xb_recv.at[rel_zh, ring, way], at_x(side))

    def yb_copy(rel_zh, ring, side):
        way = (side + 1) // 2
        there = y if ring == 0 else lax.rem(y - side + 4, 4)
        src = wt.at[group(rel_zh), there, rest]
        return remote(src, src, yb_send.at[rel_zh, ring, way], yb_recv.at[rel_zh, ring, way], at_y(side))

    def unit_columns(unit):
        return lax.rem(y + COLUMN_ORDER[unit // 2], 4)

    def wx_copy(unit, ring, side):
        way = (side + 1) // 2
        there = x if ring == 0 else lax.rem(x - side + 4, 4)
        src = wt.at[group(unit % 2), unit_columns(unit), first, there]
        return remote(src, src, wx_send.at[unit, ring, way], wx_recv.at[unit, ring, way], at_x(side))

    def wd_copy(unit):
        src = wt.at[group(unit % 2), unit_columns(unit), first]
        return remote(src, src, wd_send.at[unit], wd_recv.at[unit], other_core)

    def db_copy(unit):
        src = wt.at[group(unit % 2), unit_columns(unit), rest]
        return remote(src, src, db_send.at[unit], db_recv.at[unit], other_core)

    def both(make, *key):
        return [make(*key, side) for side in (1, -1)]

    def ring_of(make, index, ring):
        if ring == 0:
            return both(make, index, 0)
        return [make(index, 1, 1 if index % 2 == 0 else -1)]

    def start(copies):
        for copy in copies:
            copy.start()

    def recv(copies):
        for copy in copies:
            copy.wait_recv()

    def recv_other_core(unit):
        other_group = lax.rem(zh + unit % 2, 2) * 2 + 1 - core
        await_bytes(wt.at[other_group, unit_columns(unit), first], wd_recv.at[unit])

    def recv_other_rest(unit):
        other_group = lax.rem(zh + unit % 2, 2) * 2 + 1 - core
        await_bytes(wt.at[other_group, unit_columns(unit), rest], db_recv.at[unit])

    def weigh(step, index):
        rows = pl.ds(index * 2, 2)
        query = qb[step, 0, rows].reshape(2 * TOK, HEAD)
        query_tan = qb[step, 1, rows].reshape(2 * TOK, HEAD)
        key, key_tan = (kvb[step, :, :, item].reshape(16 * TOK, HEAD) for item in range(2))
        scores = lax.dot_general(query, key, NT, preferred_element_type=jnp.float32)
        top = jnp.max(scores, axis=1, keepdims=True)
        weights = jnp.exp2((scores - top) * (SCALE * LOG2E))
        score_tan = lax.dot_general(
            jnp.concatenate([query_tan, query], axis=1),
            jnp.concatenate([key, key_tan], axis=1),
            NT, preferred_element_type=jnp.float32,
        )
        moved = weights * score_tan
        total_ref[index] = jnp.sum(weights, axis=1, keepdims=True)
        spread_ref[index] = jnp.sum(moved, axis=1, keepdims=True) * SCALE
        low_ref[index] = weights.astype(jnp.bfloat16)
        moved_ref[index] = moved.astype(jnp.bfloat16)

    def sums_over(step, index, rz, cores):
        keys = pl.ds((2 * rz + cores.start) * 4 * TOK, cores.size * 4 * TOK)
        value, value_tan = (
            kvb[step, rz, cores, item].reshape(cores.size * 4 * TOK, HEAD) for item in range(2, 4)
        )
        both_values = jnp.concatenate([value, value_tan], axis=1)
        sums = jnp.dot(low_ref[index, :, keys], both_values, preferred_element_type=jnp.float32)
        return sums, jnp.dot(moved_ref[index, :, keys], value, preferred_element_type=jnp.float32)

    def attend(step, index, parts):
        sums, moved = parts[0]
        for more, more_moved in parts[1:]:
            sums, moved = sums + more, moved + more_moved
        rows = pl.ds(index * 2, 2)
        total = total_ref[index]
        plain = sums[:, :HEAD]
        carried = sums[:, HEAD:] + SCALE * moved
        attended = plain / total
        attended_tan = (carried - (spread_ref[index] / total) * plain) / total
        ob[step, rows, 0] = attended.astype(jnp.bfloat16).reshape(2, TOK, HEAD)
        ob[step, rows, 1] = attended_tan.astype(jnp.bfloat16).reshape(2, TOK, HEAD)
        start([home_copy(step, shift) for shift in ((2, 3) if index == 1 else (1,))])

    def home_copy(step, shift):
        return remote(ob.at[step, shift], ab.at[step, shift], r_send.at[step], r_recv.at[step], at_y(-shift))

    def home_wait(step):
        await_bytes(ab.at[step, pl.ds(1, 3)], r_recv.at[step])

    def product(block, step):
        left = [ob[step, 0]] + [ab[step, shift] for shift in range(1, 4)]
        left = jnp.concatenate([item.reshape(2 * TOK, HEAD) for item in left], axis=1)
        lanes = pl.ds(pl.multiple_of(step * HEAD, HEAD), HEAD)
        right = jnp.concatenate(
            [wt[lax.rem(y + shift, 4), block, :, :, :, lanes].reshape(1280, HEAD) for shift in range(4)], axis=1
        )
        return lax.dot_general(left, right, NT, preferred_element_type=jnp.float32)

    def project(first, blocks, start_step, steps):
        def one(index, carry):
            rel = first + lax.div(index, steps)
            step = start_step + lax.rem(index, steps)
            shift = rel + lax.div(rel, 2) * (5 - 2 * rel)
            block = lax.rem(y + shift, 4)
            acc[block] += product(block, step)
            return carry

        lax.fori_loop(0, blocks * steps, one, 0)

    def sends_done():
        for step in range(STEPS):
            for kind in range(3):
                heads_sent(step, kind)
            if step < 3:
                await_bytes(ob.at[step, pl.ds(1, 3)], r_send.at[step])
        copies = []
        for unit in range(8):
            for ring in range(2):
                copies += ring_of(wx_copy, unit, ring)
            copies += [wd_copy(unit), db_copy(unit)]
        for ring in range(4):
            copies += both(wz_copy, ring)
        for rel_zh in range(2):
            for ring in range(2):
                for make in (wy_copy, xb_copy, yb_copy):
                    copies += ring_of(make, rel_zh, ring)
        for half in range(2 * STEPS):
            copies.append(core_copy(half // 2, half % 2, 0))
            for hop in range(1, 5):
                if half + hop < 12:
                    copies += z_copies(half, hop)
            if half < 8:
                copies.append(core_copy(half // 2, half % 2, 1))
        for copy in copies:
            copy.wait_send()

    def x_forward(unit):
        recv(ring_of(wx_copy, unit, 0))
        start(ring_of(wx_copy, unit, 1))
        if 2 <= unit + 2 <= 7:
            start(ring_of(wx_copy, unit + 2, 0))

    def x_done(unit):
        recv(ring_of(wx_copy, unit, 1))
        wd_copy(unit).start()

    def z_arrived(half):
        if 0 <= half:
            recv(z_copies(half, 4))
            core_copy(half // 2, half % 2, 1).start()

    def pair_here(half):
        step, pair = half // 2, half % 2
        core_copy(step, pair, 0).wait_recv()
        core_copy(step, pair, 1).wait_recv()
        if pair == KEYS:
            heads_wait(step, QUERIES)

    everywhere = pl.ds(0, 2)

    def work(half, index):
        if half < 0:
            return
        step = half // 2
        if half % 2 == KEYS:
            weigh(step, index)
        else:
            attend(step, index, [sums_over(step, index, rz, everywhere) for rz in range(2)])

    def turn(at, after_first=(), after_second=(), after_last=()):
        z_own(at)
        z_forward(at - 3, 3)
        z_arrived(at - 4)
        for call in after_first:
            call()
        z_forward(at - 2, 2)
        if at >= 4:
            pair_here(at - 4)
        work(at - 4, 1)
        for call in after_second:
            call()
        z_forward(at - 1, 1)
        work(at - 4, 0)
        for call in after_last:
            call()

    def y_ring(make, ring):
        for rel_zh in range(2):
            start(ring_of(make, rel_zh, ring))

    def y_recv(make, ring):
        for rel_zh in range(2):
            recv(ring_of(make, rel_zh, ring))

    def do(call, *args):
        return lambda: call(*args)

    def wz_ring(ring):
        recv(both(wz_copy, ring - 1))
        start(both(wz_copy, ring))

    def weights_first():
        recv(both(wz_copy, 3))
        load_w.wait()
        start(ring_of(wx_copy, 0, 0))
        y_ring(wy_copy, 0)
        y_ring(xb_copy, 0)
        start(ring_of(wx_copy, 1, 0))

    def rest_to_core(*units):
        for unit in units:
            db_copy(unit).start()

    def from_core(*units):
        for unit in units:
            recv_other_core(unit)
            recv_other_rest(unit)

    def heads_more(*wanted):
        for step, pair in wanted:
            heads_start(step, pair)

    heads_start(0, KEYS)
    start(both(wz_copy, 0))
    heads_start(0, VALUES)
    acc[...] = jnp.zeros_like(acc)
    wz_ring(1)
    turn(0)
    heads_start(1, KEYS)
    wz_ring(2)
    turn(1)
    heads_start(1, VALUES)
    wz_ring(3)
    turn(2)
    heads_start(0, QUERIES)
    weights_first()
    heads_start(2, KEYS)
    turn(3, [do(heads_start, 2, VALUES)], [], [do(y_recv, wy_copy, 0), do(x_forward, 0)])
    turn(
        4,
        [do(y_ring, wy_copy, 1), do(heads_more, (3, KEYS), (3, VALUES), (1, QUERIES)), do(y_recv, xb_copy, 0)],
        [do(y_ring, xb_copy, 1), do(x_forward, 1)],
        [do(x_done, 0)],
    )
    turn(
        5,
        [do(heads_more, (4, KEYS), (4, VALUES), (2, QUERIES))],
        [do(x_forward, 2), do(x_done, 1)],
        [do(y_recv, xb_copy, 1), do(y_recv, wy_copy, 1), do(rest_to_core, 0, 1), do(y_ring, yb_copy, 0)],
    )
    turn(6, [do(heads_more, (3, QUERIES), (4, QUERIES))], [do(x_forward, 3), do(x_done, 2)], [do(x_forward, 4)])
    turn(7, [do(x_done, 3)], [do(x_done, 4)], [do(x_forward, 5)])
    turn(
        8,
        [do(y_recv, yb_copy, 0), do(y_ring, yb_copy, 1)],
        [do(rest_to_core, 2, 3, 4, 5), do(x_done, 5)],
        [do(x_forward, 6)],
    )
    turn(
        9,
        [do(x_done, 6)],
        [do(from_core, 0, 1, 2, 3, 4, 5)],
        [do(x_forward, 7), do(home_wait, 0), do(project, 0, 3, 0, 1)],
    )
    turn(
        10,
        [do(y_recv, yb_copy, 1), do(rest_to_core, 6, 7), do(x_done, 7)],
        [do(home_wait, 1)],
        [do(project, 0, 3, 1, 1)],
    )
    turn(11, [], [do(home_wait, 2)], [do(project, 0, 3, 2, 1)])
    turn(12)
    last = STEPS - 1
    core_copy(last, VALUES, 0).wait_recv()
    for index in range(2):
        sums_ref[index], carry_ref[index] = sums_over(last, index, 0, everywhere)
    z_arrived(9)
    for index in range(2):
        sums, moved = sums_over(last, index, 1, pl.ds(0, 1))
        sums_ref[index] += sums
        carry_ref[index] += moved
    core_copy(last, VALUES, 1).wait_recv()
    for index in (1, 0):
        attend(last, index, [(sums_ref[index], carry_ref[index]), sums_over(last, index, 1, pl.ds(1, 1))])
    from_core(6, 7)
    project(3, 1, 0, 3)
    home_wait(last - 1)
    project(0, 4, last - 1, 1)
    sends_done()

    home_wait(last)

    def finish(block, carry):
        columns = pl.ds(pl.multiple_of(block * 1280, 1280), 1280)
        sums = (acc[block] + product(block, last)).astype(jnp.bfloat16)
        out[0, :, columns] = sums[:TOK]
        out_t[0, :, columns] = sums[TOK:]
        return carry

    lax.fori_loop(0, 4, finish, 0)
    for half, hop in ((8, 4), (9, 3), (9, 4)):
        for copy in z_copies(half, hop):
            copy.wait_send()
    core_copy(last, KEYS, 1).wait_send()
    core_copy(last, VALUES, 1).wait_send()
    for step in (last - 1, last):
        await_bytes(ob.at[step, pl.ds(1, 3)], r_send.at[step])


def per_device(*arrays):
    dma = pltpu.SemaphoreType.DMA
    low = jnp.bfloat16
    result = pltpu.VMEM((1, TOK, 5120), low)
    anywhere = pl.BlockSpec(memory_space=pl.ANY)
    return pl.pallas_call(
        kernel,
        out_shape=(result, result),
        in_specs=[anywhere] * 7,
        out_specs=(pl.BlockSpec(memory_space=pltpu.VMEM),) * 2,
        scratch_shapes=[
            pltpu.VMEM((2 * STEPS, 3, 2, 4, TOK, HEAD), low),
            pltpu.VMEM((STEPS, 2, 2, 4, 4, TOK, HEAD), low),
            pltpu.VMEM((STEPS, 2, 4, TOK, HEAD), low),
            pltpu.VMEM((STEPS, 4, 2, TOK, HEAD), low),
            pltpu.VMEM((STEPS, 4, 2, TOK, HEAD), low),
            pltpu.VMEM((4, 4, 4, 4, 80, 640), low),
            pltpu.VMEM((4, 2 * TOK, 1280), jnp.float32),
            pltpu.VMEM((2, 2 * TOK, 16 * TOK), low),
            pltpu.VMEM((2, 2 * TOK, 16 * TOK), low),
            pltpu.VMEM((2, 2 * TOK, 1), jnp.float32),
            pltpu.VMEM((2, 2 * TOK, 1), jnp.float32),
            pltpu.VMEM((2, 2 * TOK, 2 * HEAD), jnp.float32),
            pltpu.VMEM((2, 2 * TOK, HEAD), jnp.float32),
            dma((STEPS, 3)), dma((STEPS, 3)),
            dma((2 * STEPS, 4, 2)), dma((2 * STEPS, 4, 2)),
            dma((2 * STEPS, 2)), dma((2 * STEPS, 2)),
            dma((STEPS,)), dma((STEPS,)),
            dma((4, 2)), dma((4, 2)),
            dma((2, 2, 2)), dma((2, 2, 2)),
            dma((8, 2, 2)), dma((8, 2, 2)),
            dma((8,)), dma((8,)),
            dma((2, 2, 2)), dma((2, 2, 2)),
            dma((2, 2, 2)), dma((2, 2, 2)),
            dma((8,)), dma((8,)),
            dma,
        ],
        compiler_params=pltpu.CompilerParams(
            collective_id=0, has_side_effects=True, vmem_limit_bytes=61 * 1024 * 1024
        ),
    )(*arrays[:6], arrays[6].T)


def solution(mesh):
    rows = P("dp", ("uly", "blk"), None)
    return jax.shard_map(
        per_device,
        mesh=mesh,
        in_specs=(rows,) * 6 + (P("uly", ("blk", "dp")),),
        out_specs=(rows, rows),
        check_vma=False,
    )
```
